128 devices in a mesh: pb: 8 (over z_hi, y), ka: 16 (over z_lo, x, core).
Axes of the slice: x: 4, y: 4, z: 4 (z_hi: 2, z_lo: 2; z = z_hi * 2 + z_lo), core: 2. Of those that a mesh axis runs over, the one named last changes fastest.
Arguments:
- queries: bfloat16 [8192, 1024], P(('pb', 'ka')), may hold values from -12 to 12
- key_rows: bfloat16 [8192, 1024], P(('ka', 'pb')), may hold values from -6 to 6
- value_rows: bfloat16 [8192, 1024], P(('ka', 'pb')), may hold values from -6 to 6
- output_rows: bfloat16 [8192, 1024], P(('pb', 'ka')), may hold values from -3 to 3
- grad_out: bfloat16 [8192, 1024], P(('pb', 'ka')), may hold values from -6 to 6
- log_sums: float32 [8192, 16], P(('pb', 'ka')), as said below
Outputs:
- grad_queries: float32 [8192, 1024], P(('pb', 'ka'))
- grad_keys: float32 [8192, 1024], P(('ka', 'pb'))
- grad_values: float32 [8192, 1024], P(('ka', 'pb'))
The draws below stay inside these ranges and needn't reach their ends.
Inputs may be any that keep to these rules, and one draw needn't show every extreme that they name: log_sums lies within half a unit of log(8192) + 2.
All inputs are finite; a program needn't handle non-finite values.
Results may differ from the reference program's by a relative error of at most 0.004.
Values may be sent and summed in bfloat16 or wider, within the bound.
A program may use at most 128 MiB of HBM per device.

```python
import jax
import jax.numpy as jnp
from jax import lax

H = 16
DH = 64
D = 1024
SEQ = 8192
N_PB = 8


def draw_log_sums(key, part):
    key = jax.random.fold_in(key, 7)
    spread = jax.random.uniform(key, (SEQ, H), jnp.float32, -0.5, 0.5)
    return jnp.log(jnp.float32(SEQ)) + 2.0 + spread


def level_of(stream_key, extent, shards, low, top_value):
    def one(dim, shards_of):
        heights = jax.random.uniform(jax.random.fold_in(jax.random.fold_in(stream_key, 6), dim), (shards_of,), jnp.float32, low / len(shards), top_value / len(shards))
        return jnp.repeat(jnp.exp(heights), extent[dim] // shards_of).reshape((-1,) + (1,) * (len(extent) - dim - 1))

    gain = one(*shards[0])
    for cut in shards[1:]:
        gain = gain * one(*cut)
    return gain


def normal_values(rng, dims, deviation, bound, shards=(), dtype=jnp.bfloat16):
    factor_of = level_of(rng, dims, shards, -0.22, 0.18) if shards else 1.0
    result = jax.random.normal(rng, dims, jnp.float32) * deviation * factor_of
    return jnp.minimum(jnp.maximum(result, -bound), bound).astype(dtype)


def setup_inputs(seed: int = 0) -> dict:
    keys = jax.random.split(jax.random.key(seed), 7)
    return {
        "queries": normal_values(keys[0], (SEQ, D), 2.0, 12.0, ((0, 128),)),
        "key_rows": normal_values(keys[1], (SEQ, D), 1.0, 6.0, ((0, 128),)),
        "value_rows": normal_values(keys[2], (SEQ, D), 1.0, 6.0, ((0, 128),)),
        "output_rows": normal_values(keys[3], (SEQ, D), 0.5, 3.0, ((0, 128),)),
        "grad_out": normal_values(keys[4], (SEQ, D), 1.0, 6.0, ((0, 128),)),
        "log_sums": draw_log_sums(jax.random.fold_in(keys[6], 71), 0),
    }


def reference(queries, key_rows, value_rows, output_rows, grad_out, log_sums):
    scaling = DH ** -0.5
    blocks = N_PB
    block_rows = SEQ // blocks

    def split_heads(source):
        return source.reshape(SEQ, H, DH).transpose(1, 0, 2)

    def join_heads(source):
        return source.transpose(1, 0, 2).reshape(SEQ, H * DH)

    delta = jnp.sum((grad_out.astype(jnp.float32) * output_rows.astype(jnp.float32)).reshape(SEQ, H, DH), axis=-1)

    def one_head(inputs):
        query_head, key_head, value_head, grad_head, sums_head, delta_head = inputs

        def step(carry, block):
            grad_keys, grad_values = carry
            query_part, grad_part, sums_part, delta_part = block
            scores = jnp.dot(query_part, key_head.T, preferred_element_type=jnp.float32) * scaling
            probs = jnp.exp(scores - sums_part[:, None])
            probs_low = probs.astype(jnp.bfloat16)
            grad_values = grad_values + jnp.dot(probs_low.T, grad_part, preferred_element_type=jnp.float32)
            grad_probs = jnp.dot(grad_part, value_head.T, preferred_element_type=jnp.float32)
            grad_scores = (probs * (grad_probs - delta_part[:, None])).astype(jnp.bfloat16)
            grad_queries = jnp.dot(grad_scores, key_head, preferred_element_type=jnp.float32) * scaling
            grad_keys = grad_keys + jnp.dot(grad_scores.T, query_part, preferred_element_type=jnp.float32) * scaling
            return (grad_keys, grad_values), grad_queries

        start = (jnp.zeros((SEQ, DH), jnp.float32), jnp.zeros((SEQ, DH), jnp.float32))
        sliced = (query_head.reshape(blocks, block_rows, DH), grad_head.reshape(blocks, block_rows, DH),
                  sums_head.reshape(blocks, block_rows), delta_head.reshape(blocks, block_rows))
        (grad_keys, grad_values), grad_queries = lax.scan(step, start, sliced)
        return grad_queries.reshape(SEQ, DH), grad_keys, grad_values

    grad_queries, grad_keys, grad_values = lax.map(one_head, (split_heads(queries), split_heads(key_rows), split_heads(value_rows), split_heads(grad_out), log_sums.T, delta.T))
    return join_heads(grad_queries), join_heads(grad_keys), join_heads(grad_values)
```

```python
import functools

import jax
import jax.numpy as jnp
from jax import lax
from jax.experimental import pallas as pl
from jax.experimental.pallas import tpu as pltpu
from jax.sharding import PartitionSpec as P

BF = jnp.bfloat16
F32 = jnp.float32
MESH = pl.DeviceIdType.MESH

ROWS = 64
PAIR = 128
HEAD = 64
GROUP = 8
RING = 4
CHUNK = GROUP * ROWS
SIDE = 2 * ROWS + 16
OFFSETS = (0, 1, -1, 2)
SLOT_AT = {0: 0, -1: 1, 1: 2, 2: 3}
STEPS = RING * RING


def dot_nn(a, b):
    return jnp.dot(a, b, preferred_element_type=F32)


def dot_nt(a, b):
    return lax.dot_general(a, b, (((1,), (1,)), ((), ())), preferred_element_type=F32)


def split3(value):
    high = value.astype(BF)
    rest = value - high.astype(F32)
    mid = rest.astype(BF)
    low = (rest - mid.astype(F32)).astype(BF)
    return high, mid, low


def select_rows(matrix, value):
    high, mid, low = split3(value)
    return dot_nt(matrix, high) + dot_nt(matrix, mid) + dot_nt(matrix, low)


def kernel(
    q_in, k_in, v_in, o_in, g_in, sums_in,
    dq_out, dk_out, dv_out,
    stage_q, stage_k, qbuf, kbuf, qm, gm, kt, terms,
    dq_acc, dk_acc, dv_acc, kv_send, kv_recv, q_send, q_recv,
    back_kv, back_q, home_kv, home_q,
    in_send, in_recv, ring_send, ring_recv, sum_send, sum_recv, out_send, out_recv,
):
    pb = lax.axis_index("pb")
    ka = lax.axis_index("ka")
    y = lax.rem(pb, 4)
    z_hi = pb // 4
    me = lax.rem(ka, 8)
    z_lo = ka // 8
    z = z_hi * 2 + z_lo

    def along_x(offset):
        return (pb, z_lo * 8 + lax.rem(me + (offset + 8), 8))

    def along_y(offset):
        return (z_hi * 4 + lax.rem(y + (offset + 4), 4), ka)

    def along_z(offset):
        there = lax.rem(z + (offset + 4), 4)
        return ((there // 2) * 4 + y, lax.rem(there, 2) * 8 + me)

    barrier = pltpu.get_barrier_semaphore()
    for peer in (
        [along_x(d) for d in range(1, GROUP)]
        + [along_y(d) for d in (1, 2, 3)]
        + [along_z(d) for d in (1, 2, 3)]
    ):
        pl.semaphore_signal(barrier, inc=1, device_id=peer, device_id_type=MESH)

    def remote(src, dst, send, recv, peer):
        return pltpu.make_async_remote_copy(
            src_ref=src, dst_ref=dst, send_sem=send, recv_sem=recv,
            device_id=peer, device_id_type=MESH,
        )

    def in_copy(side, d):
        stage, buf = ((stage_q, qbuf), (stage_k, kbuf))[side]
        return remote(
            stage.at[lax.rem(me + d, GROUP)], buf.at[0, d],
            in_send.at[side, d], in_recv.at[side, d], along_x(d),
        )

    def ring_copy(side, offset):
        buf, along = ((qbuf, along_y), (kbuf, along_z))[side]
        slot = SLOT_AT[offset]
        return remote(
            buf.at[0], buf.at[slot],
            ring_send.at[side, slot], ring_recv.at[side, slot], along(offset),
        )

    def forward_copy(side, half):
        buf, along = ((qbuf, along_y), (kbuf, along_z))[side]
        part = pl.ds(half * (GROUP // 2), GROUP // 2)
        index = 3 if half == 0 else 0
        return remote(
            buf.at[1 + half, part], buf.at[3, part],
            ring_send.at[side, index], ring_recv.at[side, index], along((-1, 1)[half]),
        )

    def kv_copy(slot):
        return remote(
            kv_send.at[slot - 1], kv_recv.at[slot - 1],
            sum_send.at[0, slot], sum_recv.at[0, slot], along_z(OFFSETS[slot]),
        )

    def q_copy(slot):
        return remote(
            q_send.at[slot - 1], q_recv.at[slot - 1],
            sum_send.at[1, slot], sum_recv.at[1, slot], along_y(OFFSETS[slot]),
        )

    def out_copy(side, d):
        back, home = ((back_q, home_q), (back_kv, home_kv))[side]
        return remote(
            back.at[d], home.at[d],
            out_send.at[side, d], out_recv.at[side, d], along_x(-d),
        )

    for p in range(GROUP):
        cols = slice(p * PAIR, (p + 1) * PAIR)
        stage_q[p, 0:ROWS] = q_in[:, cols]
        stage_q[p, ROWS : 2 * ROWS] = g_in[:, cols]
        stage_k[p, 0:ROWS] = k_in[:, cols]
        stage_k[p, ROWS : 2 * ROWS] = v_in[:, cols]

    product = g_in[...].astype(F32) * o_in[...].astype(F32)
    product = jnp.concatenate([product, product], axis=0)
    sums = jnp.concatenate([sums_in[...], sums_in[...]], axis=0)
    count = 16 * GROUP

    def row_of(shape):
        return lax.broadcasted_iota(jnp.int32, shape, 0)

    def col_of(shape):
        return lax.broadcasted_iota(jnp.int32, shape, 1)

    def pick(width, first, per_head):
        row, col = row_of((count, width)), col_of((count, width))
        kind = row % 4
        head = 2 * (row // 16) + kind - first
        hit = (row % 16 < 12) & (kind >= first) & (kind < first + 2) & (col // per_head == head)
        return jnp.where(hit, 1.0, 0.0).astype(BF)

    value = select_rows(pick(GROUP * PAIR, 2, HEAD), product) + select_rows(pick(16, 0, 1), sums)
    high = value.astype(BF).astype(F32)
    mid = (value - high).astype(BF).astype(F32)
    low = value - high - mid
    row, col = row_of((count, PAIR)), col_of((count, PAIR))
    third = (row % 16) // 4
    value = jnp.where(third == 0, high, jnp.where(third == 1, mid, low))
    value = jnp.where(col // ROWS == (row // 16 + me) % 2, value, 0.0).astype(BF)
    for p in range(GROUP):
        stage_q[p, 2 * ROWS : SIDE] = value[16 * p : 16 * (p + 1)]

    pl.semaphore_wait(barrier, 13)
    for d in (4, 5, 3, 2, 6, 7, 1):
        in_copy(1, d).start()
        in_copy(0, d).start()
    kbuf[0, 0] = stage_k[me]
    qbuf[0, 0] = stage_q[me]
    dq_acc[...] = jnp.zeros_like(dq_acc)
    dk_acc[...] = jnp.zeros_like(dk_acc)
    dv_acc[...] = jnp.zeros_like(dv_acc)

    lane = lax.broadcasted_iota(jnp.int32, (1, PAIR), 1)

    def prepare_q(slot):
        q = qbuf[slot, :, 0:ROWS, :].reshape(CHUNK, PAIR).astype(F32)
        g = qbuf[slot, :, ROWS : 2 * ROWS, :].reshape(CHUNK, PAIR).astype(F32)
        for h in range(2):
            own = jnp.where(lane // HEAD == h, 1.0, 0.0).astype(F32)
            qm[slot, h] = (q * (own * HEAD**-0.5)).astype(BF)
            gm[slot, h] = (g * own).astype(BF)
        for i in range(GROUP // 2):
            part = qbuf[slot, 2 * i, 2 * ROWS : SIDE, :].astype(F32)
            part += qbuf[slot, 2 * i + 1, 2 * ROWS : SIDE, :].astype(F32)
            terms[slot, 0:4, i * PAIR : (i + 1) * PAIR] = part[0:4] + part[4:8] + part[8:12]

    def prepare_k(slot):
        k = kbuf[slot, :, 0:ROWS, :].reshape(CHUNK, PAIR).astype(F32)
        kt[slot] = (k * HEAD**-0.5).T.astype(BF)

    for d in range(1, GROUP):
        in_copy(1, d).wait_recv()
    ring_copy(1, 1).start()
    ring_copy(1, -1).start()
    for d in range(1, GROUP):
        in_copy(0, d).wait_recv()
    ring_copy(0, 1).start()
    ring_copy(0, -1).start()
    prepare_k(0)
    prepare_q(0)

    def tile(kslot, qslot):
        k = kbuf[kslot, :, 0:ROWS, :].reshape(CHUNK, PAIR)
        v = kbuf[kslot, :, ROWS : 2 * ROWS, :].reshape(CHUNK, PAIR)
        for h in range(2):
            q = qm[qslot, h]
            g = gm[qslot, h]
            probs = jnp.exp(dot_nt(k, q) - terms[qslot, h : h + 1, :])
            grad = probs * (dot_nt(v, g) - terms[qslot, 2 + h : 3 + h, :])
            grad = grad.astype(BF)
            dv_acc[kslot] += dot_nn(probs.astype(BF), g)
            dk_acc[kslot] += dot_nn(grad, q)
            rows = slice(h * HEAD, (h + 1) * HEAD)
            dq_acc[qslot, rows, :] += dot_nn(kt[kslot, rows, :], grad)

    def send_kv(slot):
        kv_send[slot - 1, 0] = dk_acc[slot].astype(BF)
        kv_send[slot - 1, 1] = dv_acc[slot].astype(BF)
        kv_copy(slot).start()

    def send_q(slot):
        q_send[slot - 1] = dq_acc[slot].T.astype(BF)
        q_copy(slot).start()

    def step(t, carry):
        turn = (t + 3) // 4
        last = t // 13
        kslot = (turn + (turn // 2) * (1 - turn // 4) - 2 * (turn // 3) * (1 - turn // 4)) % 4
        place = ((t + 3) % 4) * ((t + 15) // 16)
        qslot = (1 - last) * place + last * ((place + 2) % 3 + 1)

        @pl.when(t == 1)
        def _():
            ring_copy(1, -1).wait_recv()
            forward_copy(1, 0).start()
            ring_copy(1, 1).wait_recv()
            forward_copy(1, 1).start()
            ring_copy(0, -1).wait_recv()
            forward_copy(0, 0).start()
            ring_copy(0, 1).wait_recv()
            forward_copy(0, 1).start()
            prepare_k(1)
            prepare_k(2)
            prepare_q(1)
            prepare_q(2)

        @pl.when(t == 4)
        def _():
            forward_copy(0, 0).wait_recv()
            forward_copy(0, 1).wait_recv()
            prepare_q(3)

        @pl.when(t == 5)
        def _():
            forward_copy(1, 0).wait_recv()
            forward_copy(1, 1).wait_recv()
            prepare_k(3)
            send_kv(1)

        @pl.when(t == 9)
        def _():
            send_kv(3)

        @pl.when(t == 13)
        def _():
            send_kv(2)

        @pl.when(t == 14)
        def _():
            send_q(3)

        @pl.when(t == 15)
        def _():
            send_q(1)

        tile(kslot, qslot)
        return carry

    lax.fori_loop(0, STEPS, step, 0)
    send_q(2)

    for slot in (1, 3, 2):
        kv_copy(slot).wait_recv()
    for i, acc in enumerate((dk_acc, dv_acc)):
        total = acc[0]
        for slot in (1, 2, 3):
            total = total + kv_recv[slot - 1, i].astype(F32)
        acc[0] = total
        for d in range(1, GROUP):
            back_kv[d, i] = total[d * ROWS : (d + 1) * ROWS].astype(BF)
    for d in (4, 5, 3, 2, 6, 7, 1):
        out_copy(1, d).start()
    for slot in (3, 1, 2):
        q_copy(slot).wait_recv()
    total = dq_acc[0].T
    for slot in (1, 2, 3):
        total = total + q_recv[slot - 1].astype(F32)
    for d in range(1, GROUP):
        back_q[d] = total[d * ROWS : (d + 1) * ROWS].astype(BF)
    for d in (4, 5, 3, 2, 6, 7, 1):
        out_copy(0, d).start()

    def columns(d):
        return pl.ds(pl.multiple_of(lax.rem(me + d, GROUP) * PAIR, PAIR), PAIR)

    dk_out[:, columns(0)] = dk_acc[0, 0:ROWS]
    dv_out[:, columns(0)] = dv_acc[0, 0:ROWS]
    dq_out[:, columns(0)] = total[0:ROWS]
    for d in range(1, GROUP):
        out_copy(1, d).wait_recv()
        dk_out[:, columns(d)] = home_kv[d, 0].astype(F32)
        dv_out[:, columns(d)] = home_kv[d, 1].astype(F32)
    for d in range(1, GROUP):
        out_copy(0, d).wait_recv()
        dq_out[:, columns(d)] = home_q[d].astype(F32)

    for side in range(2):
        for d in range(1, GROUP):
            in_copy(side, d).wait_send()
            out_copy(side, d).wait_send()
        ring_copy(side, 1).wait_send()
        ring_copy(side, -1).wait_send()
        forward_copy(side, 0).wait_send()
        forward_copy(side, 1).wait_send()
    for slot in (1, 2, 3):
        kv_copy(slot).wait_send()
        q_copy(slot).wait_send()


def shards(queries, key_rows, value_rows, output_rows, grad_out, log_sums):
    vmem = pl.BlockSpec(memory_space=pltpu.VMEM)
    out = jax.ShapeDtypeStruct((ROWS, GROUP * PAIR), F32)
    dma = pltpu.SemaphoreType.DMA
    return pl.pallas_call(
        kernel,
        out_shape=(out, out, out),
        in_specs=[vmem] * 6,
        out_specs=(vmem, vmem, vmem),
        scratch_shapes=[
            pltpu.VMEM((GROUP, SIDE, PAIR), BF),
            pltpu.VMEM((GROUP, 2 * ROWS, PAIR), BF),
            pltpu.VMEM((RING, GROUP, SIDE, PAIR), BF),
            pltpu.VMEM((RING, GROUP, 2 * ROWS, PAIR), BF),
            pltpu.VMEM((RING, 2, CHUNK, PAIR), BF),
            pltpu.VMEM((RING, 2, CHUNK, PAIR), BF),
            pltpu.VMEM((RING, PAIR, CHUNK), BF),
            pltpu.VMEM((RING, 8, CHUNK), F32),
            pltpu.VMEM((RING, PAIR, CHUNK), F32),
            pltpu.VMEM((RING, CHUNK, PAIR), F32),
            pltpu.VMEM((RING, CHUNK, PAIR), F32),
            pltpu.VMEM((3, 2, CHUNK, PAIR), BF),
            pltpu.VMEM((3, 2, CHUNK, PAIR), BF),
            pltpu.VMEM((3, CHUNK, PAIR), BF),
            pltpu.VMEM((3, CHUNK, PAIR), BF),
            pltpu.VMEM((GROUP, 2, ROWS, PAIR), BF),
            pltpu.VMEM((GROUP, ROWS, PAIR), BF),
            pltpu.VMEM((GROUP, 2, ROWS, PAIR), BF),
            pltpu.VMEM((GROUP, ROWS, PAIR), BF),
            dma((2, GROUP)), dma((2, GROUP)),
            dma((2, 4)), dma((2, 4)),
            dma((2, 4)), dma((2, 4)),
            dma((2, GROUP)), dma((2, GROUP)),
        ],
        compiler_params=pltpu.CompilerParams(
            collective_id=0, has_side_effects=True, vmem_limit_bytes=48 * 2**20
        ),
        cost_estimate=pl.CostEstimate(
            flops=5 * 2**30, bytes_accessed=2**21, transcendentals=2**23
        ),
    )(queries, key_rows, value_rows, output_rows, grad_out, log_sums)


def solution(mesh):
    q_side = P(("pb", "ka"), None)
    k_side = P(("ka", "pb"), None)
    return jax.shard_map(
        shards,
        mesh=mesh,
        in_specs=(q_side, k_side, k_side, q_side, q_side, q_side),
        out_specs=(q_side, k_side, k_side),
        check_vma=False,
    )
```

```python
import functools

import jax
import jax.numpy as jnp
from jax import lax
from jax.experimental import pallas as pl
from jax.experimental.pallas import tpu as pltpu
from jax.sharding import PartitionSpec as P

BF = jnp.bfloat16
F32 = jnp.float32
MESH = pl.DeviceIdType.MESH

ROWS = 64
PAIR = 128
HEAD = 64
GROUP = 8
RING = 4
CHUNK = 2 * RING * ROWS
SIDE = 2 * ROWS + 16
OFFSETS = (0, 1, -1, 2)
SLOT_AT = {1: 2, -1: 1, 2: 3}
FAR = (1, 2, 3)
STEPS = RING * RING
TILES = (
    (0, 0), (1, 0), (0, 1), (1, 1), (2, 0), (2, 1), (2, 2), (1, 2),
    (1, 3), (2, 3), (3, 1), (3, 2), (3, 3), (3, 0), (0, 2), (0, 3),
)
FORWARD_LAST = 3
HOP_AFTER = 4


def dot_nn(a, b):
    return jnp.dot(a, b, preferred_element_type=F32)


def dot_nt(a, b):
    return lax.dot_general(a, b, (((1,), (1,)), ((), ())), preferred_element_type=F32)


def split3(value):
    high = value.astype(BF)
    rest = value - high.astype(F32)
    mid = rest.astype(BF)
    low = (rest - mid.astype(F32)).astype(BF)
    return high, mid, low


def select_rows(dot, matrix, value):
    high, mid, low = split3(value)
    return dot(matrix, high) + dot(matrix, mid) + dot(matrix, low)


def kernel(
    q_hbm, k_hbm, v_hbm, o_hbm, g_hbm, sums_hbm,
    out_ref,
    q_in, k_in, v_in, o_in, g_in, sums_in, load_sem,
    stage_q, stage_k, qbuf, kbuf, qm, gm, kt, terms,
    dq_acc, dk_acc, dv_acc,
    ring_kv, ring_q, came_kv, came_q, back_kv, back_q, home_kv, home_q,
    near_kv, near_q, direct_kv, direct_q,
    near_sem, cross_sem, ring_sem, sum_sem, back_sem, direct_sem,
):
    loads = [
        pltpu.make_async_copy(src, dst, load_sem.at[i])
        for i, (src, dst) in enumerate((
            (k_hbm, k_in), (v_hbm, v_in), (g_hbm, g_in), (o_hbm, o_in), (sums_hbm, sums_in),
            (q_hbm, q_in),
        ))
    ]
    for load in loads:
        load.start()

    pb = lax.axis_index("pb")
    ka = lax.axis_index("ka")
    y = lax.rem(pb, 4)
    z_hi = pb // 4
    me = lax.rem(ka, 8)
    z_lo = ka // 8
    z = z_hi * 2 + z_lo

    x = me // 2
    core = lax.rem(me, 2)

    pairs = {
        (offset, other): lax.rem(x + (offset + 4), 4) * 2 + (1 - core if other else core)
        for offset in OFFSETS
        for other in (0, 1)
    }
    places = {}
    for offset in OFFSETS:
        at_y = lax.rem(y + (offset + 4), 4)
        at_z = lax.rem(z + (offset + 4), 4)
        for other in (0, 1):
            mine = z_lo * 8 + pairs[0, other]
            places["x", offset, other] = (pb, z_lo * 8 + pairs[offset, other])
            places["y", offset, other] = (z_hi * 4 + at_y, mine)
            places["z", offset, other] = (
                (at_z // 2) * 4 + y, lax.rem(at_z, 2) * 8 + pairs[0, other]
            )

    def pair_at(offset, other):
        return pairs[2 if offset == -2 else offset, other]

    def along_x(offset, other):
        return places["x", offset, other]

    def along_y(offset, other=0):
        return places["y", offset, other]

    def along_z(offset, other=0):
        return places["z", offset, other]

    rings = (along_y, along_z)

    barrier = pltpu.get_barrier_semaphore()
    for peer in [along_x(0, 1)] + [
        along(offset, other)
        for along in (along_x, along_y, along_z)
        for offset in OFFSETS[1:]
        for other in (0, 1)
    ]:
        pl.semaphore_signal(barrier, inc=1, device_id=peer, device_id_type=MESH)

    def remote(src, dst, sem, index, peer):
        return pltpu.make_async_remote_copy(
            src_ref=src, dst_ref=dst, send_sem=sem.at[(0, *index)], recv_sem=sem.at[(1, *index)],
            device_id=peer, device_id_type=MESH,
        )

    stages, bufs = (stage_q, stage_k), (qbuf, kbuf)
    backs, homes = (back_q, back_kv), (home_q, home_kv)
    partials, cames = (ring_q, ring_kv), (came_q, came_kv)
    nears, directs = (near_q, near_kv), (direct_q, direct_kv)
    others = slice(1, 8)
    afar = slice(2, 8)

    def near_copy(side, offset, other):
        piece = 2 * SLOT_AT.get(offset, 0) + other
        return remote(
            stages[side].at[pair_at(0, other)], bufs[side].at[0, piece],
            near_sem, (side,), rings[side](offset, other),
        )

    def near_all(side):
        view = bufs[side].at[0, others]
        return remote(view, view, near_sem, (side,), along_x(0, 1))

    def cross_copy(side, offset, other):
        chunk = SLOT_AT[offset]
        return remote(
            stages[side].at[pair_at(offset, other)], bufs[side].at[chunk, other],
            cross_sem, (side, chunk), along_x(offset, other),
        )

    def cross_all(side, chunk):
        view = bufs[side].at[chunk, 0:2]
        return remote(view, view, cross_sem, (side, chunk), along_x(0, 1))

    def ring_copy(side, chunk, offset):
        first = 2 * SLOT_AT[offset]
        return remote(
            bufs[side].at[chunk, 0:2], bufs[side].at[chunk, first : first + 2],
            ring_sem, (side, chunk), rings[side](offset),
        )

    def ring_all(side, chunk):
        view = bufs[side].at[chunk, afar]
        return remote(view, view, ring_sem, (side, chunk), along_x(0, 1))

    def sum_copy(side, chunk, offset):
        return remote(
            partials[side].at[chunk, OFFSETS.index(offset)],
            cames[side].at[chunk, SLOT_AT[offset]],
            sum_sem, (side, chunk), rings[side](offset),
        )

    def sum_all(side, chunk):
        view = cames[side].at[chunk, 1:4]
        return remote(view, view, sum_sem, (side, chunk), along_x(0, 1))

    def back_copy(side, chunk, other):
        piece = 2 * chunk + other
        return remote(
            backs[side].at[piece], homes[side].at[piece],
            back_sem, (side,), along_x(OFFSETS[chunk], other),
        )

    def back_all(side):
        view = homes[side].at[afar]
        return remote(view, view, back_sem, (side,), along_x(0, 1))

    def direct_copy(side, offset, other):
        return remote(
            nears[side].at[2 * OFFSETS.index(offset) + other],
            directs[side].at[2 * SLOT_AT.get(offset, 0) + other],
            direct_sem, (side,), rings[side](offset, other),
        )

    def direct_all(side):
        view = directs[side].at[others]
        return remote(view, view, direct_sem, (side,), along_x(0, 1))

    near = [(offset, other) for offset in (2, 1, -1, 0) for other in (0, 1)][:-2] + [(0, 1)]

    loads[0].wait()
    loads[1].wait()
    for p in range(GROUP):
        cols = slice(p * PAIR, (p + 1) * PAIR)
        stage_k[p, 0:ROWS] = k_in[:, cols]
        stage_k[p, ROWS : 2 * ROWS] = v_in[:, cols]
    kbuf[0, 0] = stage_k[me]
    for load in loads[2:]:
        load.wait()
    for p in range(GROUP):
        cols = slice(p * PAIR, (p + 1) * PAIR)
        stage_q[p, 0:ROWS] = q_in[:, cols]
        stage_q[p, ROWS : 2 * ROWS] = g_in[:, cols]

    product = g_in[...].astype(F32) * o_in[...].astype(F32)
    product = jnp.concatenate([product, product], axis=0)
    sums = jnp.concatenate([sums_in[...], sums_in[...]], axis=1)
    count = 16 * GROUP

    def row_of(shape):
        return lax.broadcasted_iota(jnp.int32, shape, 0)

    def col_of(shape):
        return lax.broadcasted_iota(jnp.int32, shape, 1)

    def pick(width, first, per_head):
        row, col = row_of((count, width)), col_of((count, width))
        kind = row % 4
        head = 2 * (row // 16) + kind - first
        hit = (row % 16 < 12) & (kind >= first) & (kind < first + 2) & (col // per_head == head)
        return jnp.where(hit, 1.0, 0.0).astype(BF)

    value = select_rows(dot_nt, pick(GROUP * PAIR, 2, HEAD), product)
    value += select_rows(dot_nn, pick(16, 0, 1), sums)
    high = value.astype(BF).astype(F32)
    mid = (value - high).astype(BF).astype(F32)
    low = value - high - mid
    row, col = row_of((count, PAIR)), col_of((count, PAIR))
    third = (row % 16) // 4
    value = jnp.where(third == 0, high, jnp.where(third == 1, mid, low))
    value = jnp.where(col // ROWS == (row // 16 + me) % 2, value, 0.0).astype(BF)
    for p in range(GROUP):
        stage_q[p, 2 * ROWS : SIDE] = value[16 * p : 16 * (p + 1)]

    qbuf[0, 0] = stage_q[me]

    pl.semaphore_wait(barrier, 19)
    for offset, other in near:
        near_copy(1, offset, other).start()
        near_copy(0, offset, other).start()
    for offset in (1, -1):
        for other in (0, 1):
            cross_copy(1, offset, other).start()
            cross_copy(0, offset, other).start()
    dq_acc[...] = jnp.zeros_like(dq_acc)
    dk_acc[...] = jnp.zeros_like(dk_acc)
    dv_acc[...] = jnp.zeros_like(dv_acc)

    lane = lax.broadcasted_iota(jnp.int32, (1, PAIR), 1)

    def prepare_q(slot):
        q = qbuf[slot, :, 0:ROWS, :].reshape(CHUNK, PAIR)
        g = qbuf[slot, :, ROWS : 2 * ROWS, :].reshape(CHUNK, PAIR)
        for h in range(2):
            own = jnp.where(lane // HEAD == h, 1.0, 0.0)
            qm[slot, h] = q * (own * HEAD**-0.5).astype(BF)
            gm[slot, h] = g * own.astype(BF)
        for i in range(RING):
            part = qbuf[slot, 2 * i, 2 * ROWS : SIDE, :].astype(F32)
            part += qbuf[slot, 2 * i + 1, 2 * ROWS : SIDE, :].astype(F32)
            terms[slot, 0:4, i * PAIR : (i + 1) * PAIR] = part[0:4] + part[4:8] + part[8:12]

    def prepare_k(slot):
        k = kbuf[slot, :, 0:ROWS, :].reshape(CHUNK, PAIR).astype(F32)
        kt[slot] = (k * HEAD**-0.5).T.astype(BF)

    def pass_on(chunk):
        for side in (1, 0):
            cross_all(side, chunk).wait_recv()
            for offset in OFFSETS[1:]:
                ring_copy(side, chunk, offset).start()

    def arrive(side, chunk):
        (near_all(side) if chunk == 0 else ring_all(side, chunk)).wait_recv()
        (prepare_q, prepare_k)[side](chunk)

    pass_on(1)
    pass_on(2)
    for other in (0, 1):
        cross_copy(1, 2, other).start()
        cross_copy(0, 2, other).start()
    arrive(1, 0)
    arrive(0, 0)

    def tile(kslot, qslot):
        k = kbuf[kslot, :, 0:ROWS, :].reshape(CHUNK, PAIR)
        v = kbuf[kslot, :, ROWS : 2 * ROWS, :].reshape(CHUNK, PAIR)
        for h in range(2):
            q = qm[qslot, h]
            g = gm[qslot, h]
            probs = jnp.exp(dot_nt(k, q) - terms[qslot, h : h + 1, :])
            grad = probs * (dot_nt(v, g) - terms[qslot, 2 + h : 3 + h, :])
            grad = grad.astype(BF)
            dv_acc[kslot] += dot_nn(probs.astype(BF), g)
            dk_acc[kslot] += dot_nn(grad, q)
            rows = slice(h * HEAD, (h + 1) * HEAD)
            dq_acc[qslot, rows, :] += dot_nn(kt[kslot, rows, :], grad)

    half = 2 * ROWS

    def send_sums(side, chunk):
        if side:
            for slot in FAR:
                rows = slice(slot * half, (slot + 1) * half)
                ring_kv[chunk, slot, 0] = dk_acc[chunk, rows].astype(BF)
                ring_kv[chunk, slot, 1] = dv_acc[chunk, rows].astype(BF)
        else:
            for slot in FAR:
                rows = slice(slot * half, (slot + 1) * half)
                ring_q[chunk, slot] = dq_acc[chunk, :, rows].T.astype(BF)
        for offset in OFFSETS[1:]:
            sum_copy(side, chunk, offset).start()

    def hop(side, chunk):
        sum_all(side, chunk).wait_recv()
        if side:
            for i, acc in enumerate((dk_acc, dv_acc)):
                total = acc[chunk, 0:half]
                for slot in FAR:
                    total = total + came_kv[chunk, slot, i].astype(F32)
                for other in (0, 1):
                    rows = slice(other * ROWS, (other + 1) * ROWS)
                    back_kv[2 * chunk + other, i] = total[rows].astype(BF)
        else:
            total = dq_acc[chunk, :, 0:half].T
            for slot in FAR:
                total = total + came_q[chunk, slot].astype(F32)
            for other in (0, 1):
                back_q[2 * chunk + other] = total[other * ROWS : (other + 1) * ROWS].astype(BF)
        for other in (0, 1):
            back_copy(side, chunk, other).start()

    def send_direct(side):
        for slot in range(RING):
            for other in (0, 1):
                first = slot * half + other * ROWS
                rows = slice(first, first + ROWS)
                if side:
                    near_kv[2 * slot + other, 0] = dk_acc[0, rows].astype(BF)
                    near_kv[2 * slot + other, 1] = dv_acc[0, rows].astype(BF)
            if not side:
                total = dq_acc[0, :, slot * half : (slot + 1) * half].T.astype(BF)
                near_q[2 * slot] = total[0:ROWS]
                near_q[2 * slot + 1] = total[ROWS:half]
        for offset, other in near:
            direct_copy(side, offset, other).start()

    events = {FORWARD_LAST: [(pass_on, (3,))]}
    seen = {(0, 0), (1, 0)}
    left = {(side, chunk): RING for side in range(2) for chunk in range(RING)}
    for i, order in enumerate(TILES):
        for side in (1, 0):
            chunk = order[1 - side]
            if (side, chunk) not in seen:
                seen.add((side, chunk))
                events.setdefault(i, []).append((arrive, (side, chunk)))
            left[side, chunk] -= 1
            if not left[side, chunk]:
                if chunk:
                    events.setdefault(i + 1, []).append((send_sums, (side, chunk)))
                    after = min(i + 1 + HOP_AFTER, STEPS + 1)
                    events.setdefault(after, []).append((hop, (side, chunk)))
                else:
                    events.setdefault(i + 1, []).append((send_direct, (side,)))

    def run(i):
        for act, operands in events.get(i, []):
            act(*operands)

    def step(t, carry):
        kslot = sum(jnp.where(t == i, order[0], 0) for i, order in enumerate(TILES))
        qslot = sum(jnp.where(t == i, order[1], 0) for i, order in enumerate(TILES))
        for i in sorted(events):
            if i < STEPS:
                pl.when(t == i)(functools.partial(run, i))
        tile(kslot, qslot)
        return carry

    lax.fori_loop(0, STEPS, step, 0)
    run(STEPS)
    run(STEPS + 1)

    def columns(offset, other):
        return pl.ds(pl.multiple_of(pair_at(offset, other) * PAIR, PAIR), PAIR)

    for side in (1, 0):
        back_all(side).wait_recv()
    for chunk in FAR:
        for other in (0, 1):
            cols = columns(-OFFSETS[chunk], other)
            piece = 2 * chunk + other
            out_ref[1, :, cols] = home_kv[piece, 0]
            out_ref[2, :, cols] = home_kv[piece, 1]
            out_ref[0, :, cols] = home_q[piece]
    for side in (0, 1):
        direct_all(side).wait_recv()

    def own_sum(first, parts):
        for part in parts:
            first = first + part.astype(F32)
        return first.astype(BF)

    cols = columns(0, 0)
    out_ref[0, :, cols] = own_sum(
        dq_acc[0, :, 0:half].T[0:ROWS], [direct_q[2 * slot] for slot in FAR]
    )
    for i, acc in enumerate((dk_acc, dv_acc)):
        out_ref[1 + i, :, cols] = own_sum(
            acc[0, 0:ROWS], [direct_kv[2 * slot, i] for slot in FAR]
        )
    cols = columns(0, 1)
    out_ref[0, :, cols] = own_sum(
        direct_q[1].astype(F32), [direct_q[2 * slot + 1] for slot in FAR]
    )
    for i in range(2):
        out_ref[1 + i, :, cols] = own_sum(
            direct_kv[1, i].astype(F32), [direct_kv[2 * slot + 1, i] for slot in FAR]
        )

    for side in range(2):
        near_all(side).wait_send()
        back_all(side).wait_send()
        direct_all(side).wait_send()
        for chunk in FAR:
            cross_all(side, chunk).wait_send()
            ring_all(side, chunk).wait_send()
            sum_all(side, chunk).wait_send()


def shards(queries, key_rows, value_rows, output_rows, grad_out, log_sums):
    vmem = pl.BlockSpec(memory_space=pltpu.VMEM)
    hbm = pl.BlockSpec(memory_space=pltpu.HBM)
    out = jax.ShapeDtypeStruct((ROWS, GROUP * PAIR), F32)
    dma = pltpu.SemaphoreType.DMA
    r = pl.pallas_call(
        kernel,
        out_shape=jax.ShapeDtypeStruct((3, ROWS, GROUP * PAIR), BF),
        in_specs=[hbm] * 6,
        out_specs=vmem,
        scratch_shapes=[pltpu.VMEM((ROWS, GROUP * PAIR), BF)] * 5 + [
            pltpu.VMEM((2 * GROUP, ROWS), F32),
            dma((6,)),
            pltpu.VMEM((GROUP, SIDE, PAIR), BF),
            pltpu.VMEM((GROUP, 2 * ROWS, PAIR), BF),
            pltpu.VMEM((RING, GROUP, SIDE, PAIR), BF),
            pltpu.VMEM((RING, GROUP, 2 * ROWS, PAIR), BF),
            pltpu.VMEM((RING, 2, CHUNK, PAIR), BF),
            pltpu.VMEM((RING, 2, CHUNK, PAIR), BF),
            pltpu.VMEM((RING, PAIR, CHUNK), BF),
            pltpu.VMEM((RING, 8, CHUNK), F32),
            pltpu.VMEM((RING, PAIR, CHUNK), F32),
            pltpu.VMEM((RING, CHUNK, PAIR), F32),
            pltpu.VMEM((RING, CHUNK, PAIR), F32),
            pltpu.VMEM((RING, RING, 2, 2 * ROWS, PAIR), BF),
            pltpu.VMEM((RING, RING, 2 * ROWS, PAIR), BF),
            pltpu.VMEM((RING, RING, 2, 2 * ROWS, PAIR), BF),
            pltpu.VMEM((RING, RING, 2 * ROWS, PAIR), BF),
            pltpu.VMEM((GROUP, 2, ROWS, PAIR), BF),
            pltpu.VMEM((GROUP, ROWS, PAIR), BF),
            pltpu.VMEM((GROUP, 2, ROWS, PAIR), BF),
            pltpu.VMEM((GROUP, ROWS, PAIR), BF),
            pltpu.VMEM((GROUP, 2, ROWS, PAIR), BF),
            pltpu.VMEM((GROUP, ROWS, PAIR), BF),
            pltpu.VMEM((GROUP, 2, ROWS, PAIR), BF),
            pltpu.VMEM((GROUP, ROWS, PAIR), BF),
            dma((2, 2)),
            dma((2, 2, RING)),
            dma((2, 2, RING)),
            dma((2, 2, RING)),
            dma((2, 2)),
            dma((2, 2)),
        ],
        compiler_params=pltpu.CompilerParams(
            collective_id=0, has_side_effects=True, vmem_limit_bytes=56 * 2**20
        ),
        cost_estimate=pl.CostEstimate(
            flops=5 * 2**30, bytes_accessed=2**21, transcendentals=2**23
        ),
    )(queries, key_rows, value_rows, output_rows, grad_out, log_sums.T)
    return r[0].astype(F32), r[1].astype(F32), r[2].astype(F32)


def solution(mesh):
    q_side = P(("pb", "ka"), None)
    k_side = P(("ka", "pb"), None)
    return jax.shard_map(
        shards,
        mesh=mesh,
        in_specs=(q_side, k_side, k_side, q_side, q_side, q_side),
        out_specs=(q_side, k_side, k_side),
        check_vma=False,
    )
```

```python
import functools

import jax
import jax.numpy as jnp
from jax import lax
from jax.experimental import pallas as pl
from jax.experimental.pallas import tpu as pltpu
from jax.sharding import PartitionSpec as P

BF = jnp.bfloat16
F32 = jnp.float32
MESH = pl.DeviceIdType.MESH

ROWS = 64
PAIR = 128
HEAD = 64
GROUP = 8
RING = 4
CHUNK = 2 * RING * ROWS
SIDE = 2 * ROWS + 16
OFFSETS = (0, 1, -1, 2)
SLOT_AT = {1: 2, -1: 1, 2: 3}
FAR = (1, 2, 3)
STEPS = RING * RING
TILES = (
    (0, 0), (1, 0), (1, 1), (2, 0), (2, 1), (2, 2), (1, 2), (1, 3),
    (2, 3), (0, 3), (3, 3), (3, 0), (3, 1), (3, 2), (0, 1), (0, 2),
)
FORWARD_AT = {2: 1, 3: 2}
HOP_AFTER = 5


def dot_nn(a, b):
    return jnp.dot(a, b, preferred_element_type=F32)


def dot_nt(a, b):
    return lax.dot_general(a, b, (((1,), (1,)), ((), ())), preferred_element_type=F32)


def split3(value):
    high = value.astype(BF)
    rest = value - high.astype(F32)
    mid = rest.astype(BF)
    low = (rest - mid.astype(F32)).astype(BF)
    return high, mid, low


def select_rows(dot, matrix, value):
    high, mid, low = split3(value)
    return dot(matrix, high) + dot(matrix, mid) + dot(matrix, low)


def kernel(
    q_hbm, k_hbm, v_hbm, o_hbm, g_hbm, sums_hbm,
    out_ref,
    q_in, k_in, v_in, o_in, g_in, sums_in, load_sem,
    stage_q, stage_k, qbuf, kbuf, qm, gm, kt, terms,
    dq_acc, dk_acc, dv_acc,
    ring_kv, came_kv, back_kv, home_kv, near_kv, direct_kv, send_q, came_q, own_q,
    near_sem, cross_sem, ring_sem, sum_sem, back_sem, direct_sem, query_sem,
):
    loads = [
        pltpu.make_async_copy(src, dst, load_sem.at[i])
        for i, (src, dst) in enumerate((
            (k_hbm, k_in), (v_hbm, v_in), (g_hbm, g_in), (o_hbm, o_in), (sums_hbm, sums_in),
            (q_hbm, q_in),
        ))
    ]
    for load in loads:
        load.start()

    pb = lax.axis_index("pb")
    ka = lax.axis_index("ka")
    y = lax.rem(pb, 4)
    z_hi = pb // 4
    me = lax.rem(ka, 8)
    z_lo = ka // 8
    z = z_hi * 2 + z_lo

    x = me // 2
    core = lax.rem(me, 2)

    pairs = {
        (offset, other): lax.rem(x + (offset + 4), 4) * 2 + (1 - core if other else core)
        for offset in OFFSETS
        for other in (0, 1)
    }
    places = {}
    for offset in OFFSETS:
        at_y = lax.rem(y + (offset + 4), 4)
        at_z = lax.rem(z + (offset + 4), 4)
        for other in (0, 1):
            mine = z_lo * 8 + pairs[0, other]
            places["x", offset, other] = (pb, z_lo * 8 + pairs[offset, other])
            places["y", offset, other] = (z_hi * 4 + at_y, mine)
            for chunk in FAR:
                places["xy", chunk, offset, other] = (
                    z_hi * 4 + at_y, z_lo * 8 + pairs[OFFSETS[chunk], other]
                )
            places["z", offset, other] = (
                (at_z // 2) * 4 + y, lax.rem(at_z, 2) * 8 + pairs[0, other]
            )

    def pair_at(offset, other):
        return pairs[2 if offset == -2 else offset, other]

    def along_x(offset, other):
        return places["x", offset, other]

    def along_y(offset, other=0):
        return places["y", offset, other]

    def along_z(offset, other=0):
        return places["z", offset, other]

    rings = (along_y, along_z)

    barrier = pltpu.get_barrier_semaphore()
    for peer in [along_x(0, 1)] + [
        along(offset, other)
        for along in (along_x, along_y, along_z)
        for offset in OFFSETS[1:]
        for other in (0, 1)
    ]:
        pl.semaphore_signal(barrier, inc=1, device_id=peer, device_id_type=MESH)

    def remote(src, dst, sem, index, peer):
        return pltpu.make_async_remote_copy(
            src_ref=src, dst_ref=dst, send_sem=sem.at[(0, *index)], recv_sem=sem.at[(1, *index)],
            device_id=peer, device_id_type=MESH,
        )

    stages, bufs = (stage_q, stage_k), (qbuf, kbuf)
    others = slice(1, 8)
    afar = slice(2, 8)

    def near_copy(side, offset, other):
        piece = 2 * SLOT_AT.get(offset, 0) + other
        return remote(
            stages[side].at[pair_at(0, other)], bufs[side].at[0, piece],
            near_sem, (side,), rings[side](offset, other),
        )

    def near_all(side):
        view = bufs[side].at[0, others]
        return remote(view, view, near_sem, (side,), along_x(0, 1))

    def cross_copy(side, offset, other):
        chunk = SLOT_AT[offset]
        return remote(
            stages[side].at[pair_at(offset, other)], bufs[side].at[chunk, other],
            cross_sem, (side, chunk), along_x(offset, other),
        )

    def cross_all(side, chunk):
        view = bufs[side].at[chunk, 0:2]
        return remote(view, view, cross_sem, (side, chunk), along_x(0, 1))

    def ring_copy(side, chunk, offset):
        first = 2 * SLOT_AT[offset]
        return remote(
            bufs[side].at[chunk, 0:2], bufs[side].at[chunk, first : first + 2],
            ring_sem, (side, chunk), rings[side](offset),
        )

    def ring_all(side, chunk):
        view = bufs[side].at[chunk, afar]
        return remote(view, view, ring_sem, (side, chunk), along_x(0, 1))

    def sum_copy(chunk, offset):
        return remote(
            ring_kv.at[chunk, OFFSETS.index(offset)], came_kv.at[chunk, SLOT_AT[offset]],
            sum_sem, (chunk,), along_z(offset),
        )

    def sum_all(chunk):
        view = came_kv.at[chunk, 1:4]
        return remote(view, view, sum_sem, (chunk,), along_x(0, 1))

    def back_copy(chunk, other):
        piece = 2 * chunk + other
        return remote(
            back_kv.at[piece], home_kv.at[piece],
            back_sem, (), along_x(OFFSETS[chunk], other),
        )

    def back_all():
        view = home_kv.at[afar]
        return remote(view, view, back_sem, (), along_x(0, 1))

    def direct_copy(offset, other):
        return remote(
            near_kv.at[2 * OFFSETS.index(offset) + other],
            direct_kv.at[2 * SLOT_AT.get(offset, 0) + other],
            direct_sem, (), along_z(offset, other),
        )

    def direct_all():
        view = direct_kv.at[others]
        return remote(view, view, direct_sem, (), along_x(0, 1))

    def query_copy(chunk, offset, other):
        peer = places["xy", chunk, offset, other] if chunk else along_y(offset, other)
        return remote(
            send_q.at[chunk, 2 * OFFSETS.index(offset) + other],
            came_q.at[chunk, 2 * SLOT_AT.get(offset, 0) + other],
            query_sem, (chunk,), peer,
        )

    def query_all(chunk):
        view = came_q.at[chunk] if chunk else came_q.at[0, others]
        return remote(view, view, query_sem, (chunk,), along_x(0, 1))

    near = [(offset, other) for offset in (2, 1, -1, 0) for other in (0, 1)][:-2] + [(0, 1)]

    loads[0].wait()
    loads[1].wait()
    for p in range(GROUP):
        cols = slice(p * PAIR, (p + 1) * PAIR)
        stage_k[p, 0:ROWS] = k_in[:, cols]
        stage_k[p, ROWS : 2 * ROWS] = v_in[:, cols]
    kbuf[0, 0] = stage_k[me]
    for load in loads[2:]:
        load.wait()
    for p in range(GROUP):
        cols = slice(p * PAIR, (p + 1) * PAIR)
        stage_q[p, 0:ROWS] = q_in[:, cols]
        stage_q[p, ROWS : 2 * ROWS] = g_in[:, cols]

    product = g_in[...].astype(F32) * o_in[...].astype(F32)
    product = jnp.concatenate([product, product], axis=0)
    sums = jnp.concatenate([sums_in[...], sums_in[...]], axis=1)
    count = 16 * GROUP

    def row_of(shape):
        return lax.broadcasted_iota(jnp.int32, shape, 0)

    def col_of(shape):
        return lax.broadcasted_iota(jnp.int32, shape, 1)

    def pick(width, first, per_head):
        row, col = row_of((count, width)), col_of((count, width))
        kind = row % 4
        head = 2 * (row // 16) + kind - first
        hit = (row % 16 < 12) & (kind >= first) & (kind < first + 2) & (col // per_head == head)
        return jnp.where(hit, 1.0, 0.0).astype(BF)

    value = select_rows(dot_nt, pick(GROUP * PAIR, 2, HEAD), product)
    value += select_rows(dot_nn, pick(16, 0, 1), sums)
    high = value.astype(BF).astype(F32)
    mid = (value - high).astype(BF).astype(F32)
    low = value - high - mid
    row, col = row_of((count, PAIR)), col_of((count, PAIR))
    third = (row % 16) // 4
    value = jnp.where(third == 0, high, jnp.where(third == 1, mid, low))
    value = jnp.where(col // ROWS == (row // 16 + me) % 2, value, 0.0).astype(BF)
    for p in range(GROUP):
        stage_q[p, 2 * ROWS : SIDE] = value[16 * p : 16 * (p + 1)]

    qbuf[0, 0] = stage_q[me]

    pl.semaphore_wait(barrier, 19)
    for offset, other in near:
        near_copy(1, offset, other).start()
        near_copy(0, offset, other).start()
    for offset in (1, -1):
        for other in (0, 1):
            cross_copy(1, offset, other).start()
            cross_copy(0, offset, other).start()
    dq_acc[...] = jnp.zeros_like(dq_acc)
    dk_acc[...] = jnp.zeros_like(dk_acc)
    dv_acc[...] = jnp.zeros_like(dv_acc)

    lane = lax.broadcasted_iota(jnp.int32, (1, PAIR), 1)

    def prepare_q(slot):
        q = qbuf[slot, :, 0:ROWS, :].reshape(CHUNK, PAIR)
        g = qbuf[slot, :, ROWS : 2 * ROWS, :].reshape(CHUNK, PAIR)
        for h in range(2):
            own = jnp.where(lane // HEAD == h, 1.0, 0.0)
            qm[slot, h] = q * (own * HEAD**-0.5).astype(BF)
            gm[slot, h] = g * own.astype(BF)
        for i in range(RING):
            part = qbuf[slot, 2 * i, 2 * ROWS : SIDE, :].astype(F32)
            part += qbuf[slot, 2 * i + 1, 2 * ROWS : SIDE, :].astype(F32)
            terms[slot, 0:4, i * PAIR : (i + 1) * PAIR] = part[0:4] + part[4:8] + part[8:12]

    def prepare_k(slot):
        k = kbuf[slot, :, 0:ROWS, :].reshape(CHUNK, PAIR).astype(F32)
        kt[slot] = (k * HEAD**-0.5).T.astype(BF)

    def pass_on(chunk):
        for side in (1, 0):
            cross_all(side, chunk).wait_recv()
            for offset in OFFSETS[1:]:
                ring_copy(side, chunk, offset).start()

    def arrive(side, chunk):
        (near_all(side) if chunk == 0 else ring_all(side, chunk)).wait_recv()
        (prepare_q, prepare_k)[side](chunk)

    pass_on(1)
    for other in (0, 1):
        cross_copy(1, 2, other).start()
        cross_copy(0, 2, other).start()
    arrive(1, 0)
    arrive(0, 0)

    def tile(kslot, qslot):
        k = kbuf[kslot, :, 0:ROWS, :].reshape(CHUNK, PAIR)
        v = kbuf[kslot, :, ROWS : 2 * ROWS, :].reshape(CHUNK, PAIR)
        for h in range(2):
            q = qm[qslot, h]
            g = gm[qslot, h]
            probs = jnp.exp(dot_nt(k, q) - terms[qslot, h : h + 1, :])
            grad = probs * (dot_nt(v, g) - terms[qslot, 2 + h : 3 + h, :])
            grad = grad.astype(BF)
            dv_acc[kslot] += dot_nn(probs.astype(BF), g)
            dk_acc[kslot] += dot_nn(grad, q)
            rows = slice(h * HEAD, (h + 1) * HEAD)
            dq_acc[qslot, rows, :] += dot_nn(kt[kslot, rows, :], grad)

    half = 2 * ROWS

    def send_sums(chunk):
        for slot in FAR:
            rows = slice(slot * half, (slot + 1) * half)
            ring_kv[chunk, slot, 0] = dk_acc[chunk, rows].astype(BF)
            ring_kv[chunk, slot, 1] = dv_acc[chunk, rows].astype(BF)
        for offset in OFFSETS[1:]:
            sum_copy(chunk, offset).start()

    def hop(chunk):
        sum_all(chunk).wait_recv()
        for i, acc in enumerate((dk_acc, dv_acc)):
            total = acc[chunk, 0:half]
            for slot in FAR:
                total = total + came_kv[chunk, slot, i].astype(F32)
            for other in (0, 1):
                rows = slice(other * ROWS, (other + 1) * ROWS)
                back_kv[2 * chunk + other, i] = total[rows].astype(BF)
        for other in (0, 1):
            back_copy(chunk, other).start()

    def send_direct():
        for piece in range(1, GROUP):
            rows = slice(piece * ROWS, (piece + 1) * ROWS)
            near_kv[piece, 0] = dk_acc[0, rows].astype(BF)
            near_kv[piece, 1] = dv_acc[0, rows].astype(BF)
        for offset, other in near:
            direct_copy(offset, other).start()

    def send_query(chunk):
        total = dq_acc[chunk].T
        if not chunk:
            own_q[...] = total[0:ROWS]
        send_q[chunk] = total.astype(BF).reshape(GROUP, ROWS, PAIR)
        for offset, other in near + [(0, 0)] * bool(chunk):
            query_copy(chunk, offset, other).start()

    events = {}
    for chunk, i in FORWARD_AT.items():
        events.setdefault(i, []).append((pass_on, (chunk,)))
    seen = {(0, 0), (1, 0)}
    left = {(side, chunk): RING for side in range(2) for chunk in range(RING)}
    for i, order in enumerate(TILES):
        for side in (1, 0):
            chunk = order[1 - side]
            if (side, chunk) not in seen:
                seen.add((side, chunk))
                events.setdefault(i, []).append((arrive, (side, chunk)))
            left[side, chunk] -= 1
            if not left[side, chunk]:
                if not side:
                    events.setdefault(i + 1, []).append((send_query, (chunk,)))
                elif chunk:
                    events.setdefault(i + 1, []).append((send_sums, (chunk,)))
                    after = min(i + 1 + HOP_AFTER, STEPS + 1)
                    events.setdefault(after, []).append((hop, (chunk,)))
                else:
                    events.setdefault(i + 1, []).append((send_direct, ()))

    def run(i):
        for act, operands in events.get(i, []):
            act(*operands)

    def step(t, carry):
        kslot = sum(jnp.where(t == i, order[0], 0) for i, order in enumerate(TILES))
        qslot = sum(jnp.where(t == i, order[1], 0) for i, order in enumerate(TILES))
        for i in sorted(events):
            if i < STEPS:
                pl.when(t == i)(functools.partial(run, i))
        tile(kslot, qslot)
        return carry

    lax.fori_loop(0, STEPS, step, 0)
    run(STEPS)
    run(STEPS + 1)

    def columns(offset, other):
        return pl.ds(pl.multiple_of(pair_at(offset, other) * PAIR, PAIR), PAIR)

    def own_sum(first, parts):
        for part in parts:
            first = first + part.astype(F32)
        return first.astype(BF)

    back_all().wait_recv()
    for chunk in FAR:
        for other in (0, 1):
            cols = columns(-OFFSETS[chunk], other)
            piece = 2 * chunk + other
            out_ref[1, :, cols] = home_kv[piece, 0]
            out_ref[2, :, cols] = home_kv[piece, 1]
    for chunk in range(RING):
        query_all(chunk).wait_recv()
        for other in (0, 1):
            parts = [came_q[chunk, 2 * slot + other] for slot in range(RING)]
            first = parts[0].astype(F32) if chunk or other else own_q[...]
            out_ref[0, :, columns(-OFFSETS[chunk], other)] = own_sum(first, parts[1:])
    direct_all().wait_recv()
    for i, acc in enumerate((dk_acc, dv_acc)):
        for other in (0, 1):
            parts = [direct_kv[2 * slot + other, i] for slot in range(RING)]
            first = parts[0].astype(F32) if other else acc[0, 0:ROWS]
            out_ref[1 + i, :, columns(0, other)] = own_sum(first, parts[1:])

    back_all().wait_send()
    direct_all().wait_send()
    for chunk in range(RING):
        query_all(chunk).wait_send()
    for chunk in FAR:
        sum_all(chunk).wait_send()
    for side in range(2):
        near_all(side).wait_send()
        for chunk in FAR:
            cross_all(side, chunk).wait_send()
            ring_all(side, chunk).wait_send()


def shards(queries, key_rows, value_rows, output_rows, grad_out, log_sums):
    vmem = pl.BlockSpec(memory_space=pltpu.VMEM)
    hbm = pl.BlockSpec(memory_space=pltpu.HBM)
    out = jax.ShapeDtypeStruct((ROWS, GROUP * PAIR), F32)
    dma = pltpu.SemaphoreType.DMA
    r = pl.pallas_call(
        kernel,
        out_shape=jax.ShapeDtypeStruct((3, ROWS, GROUP * PAIR), BF),
        in_specs=[hbm] * 6,
        out_specs=vmem,
        scratch_shapes=[pltpu.VMEM((ROWS, GROUP * PAIR), BF)] * 5 + [
            pltpu.VMEM((2 * GROUP, ROWS), F32),
            dma((6,)),
            pltpu.VMEM((GROUP, SIDE, PAIR), BF),
            pltpu.VMEM((GROUP, 2 * ROWS, PAIR), BF),
            pltpu.VMEM((RING, GROUP, SIDE, PAIR), BF),
            pltpu.VMEM((RING, GROUP, 2 * ROWS, PAIR), BF),
            pltpu.VMEM((RING, 2, CHUNK, PAIR), BF),
            pltpu.VMEM((RING, 2, CHUNK, PAIR), BF),
            pltpu.VMEM((RING, PAIR, CHUNK), BF),
            pltpu.VMEM((RING, 8, CHUNK), F32),
            pltpu.VMEM((RING, PAIR, CHUNK), F32),
            pltpu.VMEM((RING, CHUNK, PAIR), F32),
            pltpu.VMEM((RING, CHUNK, PAIR), F32),
            pltpu.VMEM((RING, RING, 2, 2 * ROWS, PAIR), BF),
            pltpu.VMEM((RING, RING, 2, 2 * ROWS, PAIR), BF),
            pltpu.VMEM((GROUP, 2, ROWS, PAIR), BF),
            pltpu.VMEM((GROUP, 2, ROWS, PAIR), BF),
            pltpu.VMEM((GROUP, 2, ROWS, PAIR), BF),
            pltpu.VMEM((GROUP, 2, ROWS, PAIR), BF),
            pltpu.VMEM((RING, GROUP, ROWS, PAIR), BF),
            pltpu.VMEM((RING, GROUP, ROWS, PAIR), BF),
            pltpu.VMEM((ROWS, PAIR), F32),
            dma((2, 2)),
            dma((2, 2, RING)),
            dma((2, 2, RING)),
            dma((2, RING)),
            dma((2,)),
            dma((2,)),
            dma((2, RING)),
        ],
        compiler_params=pltpu.CompilerParams(
            collective_id=0, has_side_effects=True, vmem_limit_bytes=56 * 2**20
        ),
        cost_estimate=pl.CostEstimate(
            flops=5 * 2**30, bytes_accessed=2**21, transcendentals=2**23
        ),
    )(queries, key_rows, value_rows, output_rows, grad_out, log_sums.T)
    return r[0].astype(F32), r[1].astype(F32), r[2].astype(F32)


def solution(mesh):
    q_side = P(("pb", "ka"), None)
    k_side = P(("ka", "pb"), None)
    return jax.shard_map(
        shards,
        mesh=mesh,
        in_specs=(q_side, k_side, k_side, q_side, q_side, q_side),
        out_specs=(q_side, k_side, k_side),
        check_vma=False,
    )
```

```python
import jax
import jax.numpy as jnp
from jax import lax
from jax.experimental import pallas as pl
from jax.experimental.pallas import tpu as pltpu
from jax.sharding import PartitionSpec as P

BF = jnp.bfloat16
F32 = jnp.float32
MESH = pl.DeviceIdType.MESH

ROWS = 64
PAIR = 128
HEAD = 64
GROUP = 8
RING = 4
CHUNK = 2 * RING * ROWS
SIDE = 2 * ROWS + 16
OFFSETS = (0, 1, -1, 2)
SLOT_AT = {1: 2, -1: 1, 2: 3}
FAR = (1, 2, 3)
STEPS = RING * RING
TILES = (
    (0, 0), (1, 0), (1, 1), (2, 0), (2, 1), (2, 2), (1, 2), (1, 3),
    (2, 3), (0, 3), (3, 3), (3, 0), (3, 1), (3, 2), (0, 1), (0, 2),
)
FORWARD_AT = {2: 1, 3: 2}
HOP_AFTER = 5


def dot_nn(a, b):
    return jnp.dot(a, b, preferred_element_type=F32)


def dot_nt(a, b):
    return lax.dot_general(a, b, (((1,), (1,)), ((), ())), preferred_element_type=F32)


def split3(value):
    high = value.astype(BF)
    rest = value - high.astype(F32)
    mid = rest.astype(BF)
    low = (rest - mid.astype(F32)).astype(BF)
    return high, mid, low


def select_rows(dot, matrix, value):
    high, mid, low = split3(value)
    return dot(matrix, high) + dot(matrix, mid) + dot(matrix, low)


def kernel(
    q_hbm, k_hbm, v_hbm, o_hbm, g_hbm, sums_hbm,
    out_ref,
    q_in, k_in, v_in, o_in, g_in, sums_in, load_sem,
    stage_q, stage_k, qbuf, kbuf, qm, gm, kt, terms,
    dq_acc, dk_acc, dv_acc,
    ring_kv, came_kv, back_kv, home_kv, near_kv, direct_kv, send_q, came_q, own_q,
    near_sem, cross_sem, ring_sem, sum_sem, back_sem, direct_sem, query_sem,
):
    loads = [
        pltpu.make_async_copy(src, dst, load_sem.at[i])
        for i, (src, dst) in enumerate((
            (k_hbm, k_in), (v_hbm, v_in), (g_hbm, g_in), (o_hbm, o_in), (sums_hbm, sums_in),
            (q_hbm, q_in),
        ))
    ]
    for load in loads:
        load.start()

    pb = lax.axis_index("pb")
    ka = lax.axis_index("ka")
    y = lax.rem(pb, 4)
    z_hi = pb // 4
    me = lax.rem(ka, 8)
    z_lo = ka // 8
    z = z_hi * 2 + z_lo

    x = me // 2
    core = lax.rem(me, 2)

    pairs = {
        (offset, other): lax.rem(x + (offset + 4), 4) * 2 + (1 - core if other else core)
        for offset in OFFSETS
        for other in (0, 1)
    }
    places = {}
    for offset in OFFSETS:
        at_y = lax.rem(y + (offset + 4), 4)
        at_z = lax.rem(z + (offset + 4), 4)
        for other in (0, 1):
            mine = z_lo * 8 + pairs[0, other]
            places["x", offset, other] = (pb, z_lo * 8 + pairs[offset, other])
            places["y", offset, other] = (z_hi * 4 + at_y, mine)
            for chunk in FAR:
                places["xy", chunk, offset, other] = (
                    z_hi * 4 + at_y, z_lo * 8 + pairs[OFFSETS[chunk], other]
                )
            places["z", offset, other] = (
                (at_z // 2) * 4 + y, lax.rem(at_z, 2) * 8 + pairs[0, other]
            )

    def pair_at(offset, other):
        return pairs[2 if offset == -2 else offset, other]

    def along_x(offset, other):
        return places["x", offset, other]

    def along_y(offset, other=0):
        return places["y", offset, other]

    def along_z(offset, other=0):
        return places["z", offset, other]

    rings = (along_y, along_z)

    barrier = pltpu.get_barrier_semaphore()
    for peer in [along_x(0, 1)] + [
        along(offset, other)
        for along in (along_x, along_y, along_z)
        for offset in OFFSETS[1:]
        for other in (0, 1)
    ]:
        pl.semaphore_signal(barrier, inc=1, device_id=peer, device_id_type=MESH)

    def remote(src, dst, sem, index, peer):
        return pltpu.make_async_remote_copy(
            src_ref=src, dst_ref=dst, send_sem=sem.at[(0, *index)], recv_sem=sem.at[(1, *index)],
            device_id=peer, device_id_type=MESH,
        )

    stages, bufs = (stage_q, stage_k), (qbuf, kbuf)
    others = slice(1, 8)
    afar = slice(2, 8)

    def near_copy(side, offset, other):
        piece = 2 * SLOT_AT.get(offset, 0) + other
        return remote(
            stages[side].at[pair_at(0, other)], bufs[side].at[0, piece],
            near_sem, (side,), rings[side](offset, other),
        )

    def near_all(side):
        view = bufs[side].at[0, others]
        return remote(view, view, near_sem, (side,), along_x(0, 1))

    def cross_copy(side, offset, other):
        chunk = SLOT_AT[offset]
        return remote(
            stages[side].at[pair_at(offset, other)], bufs[side].at[chunk, other],
            cross_sem, (side, chunk), along_x(offset, other),
        )

    def cross_all(side, chunk):
        view = bufs[side].at[chunk, 0:2]
        return remote(view, view, cross_sem, (side, chunk), along_x(0, 1))

    def ring_copy(side, chunk, offset):
        first = 2 * SLOT_AT[offset]
        return remote(
            bufs[side].at[chunk, 0:2], bufs[side].at[chunk, first : first + 2],
            ring_sem, (side, chunk), rings[side](offset),
        )

    def ring_all(side, chunk):
        view = bufs[side].at[chunk, afar]
        return remote(view, view, ring_sem, (side, chunk), along_x(0, 1))

    def sum_copy(chunk, offset):
        return remote(
            ring_kv.at[chunk, OFFSETS.index(offset)], came_kv.at[chunk, SLOT_AT[offset]],
            sum_sem, (chunk,), along_z(offset),
        )

    def sum_all(chunk):
        view = came_kv.at[chunk, 1:4]
        return remote(view, view, sum_sem, (chunk,), along_x(0, 1))

    def back_copy(chunk, other):
        piece = 2 * chunk + other
        return remote(
            back_kv.at[piece], home_kv.at[piece],
            back_sem, (), along_x(OFFSETS[chunk], other),
        )

    def back_all():
        view = home_kv.at[afar]
        return remote(view, view, back_sem, (), along_x(0, 1))

    def direct_copy(offset, other):
        return remote(
            near_kv.at[2 * OFFSETS.index(offset) + other],
            direct_kv.at[2 * SLOT_AT.get(offset, 0) + other],
            direct_sem, (), along_z(offset, other),
        )

    def direct_all():
        view = direct_kv.at[others]
        return remote(view, view, direct_sem, (), along_x(0, 1))

    def query_copy(chunk, offset, other):
        peer = places["xy", chunk, offset, other] if chunk else along_y(offset, other)
        return remote(
            send_q.at[chunk, 2 * OFFSETS.index(offset) + other],
            came_q.at[chunk, 2 * SLOT_AT.get(offset, 0) + other],
            query_sem, (chunk,), peer,
        )

    def query_all(chunk):
        view = came_q.at[chunk] if chunk else came_q.at[0, others]
        return remote(view, view, query_sem, (chunk,), along_x(0, 1))

    near = [(offset, other) for offset in (2, 1, -1, 0) for other in (0, 1)][:-2] + [(0, 1)]

    loads[0].wait()
    loads[1].wait()
    for p in range(GROUP):
        cols = slice(p * PAIR, (p + 1) * PAIR)
        stage_k[p, 0:ROWS] = k_in[:, cols]
        stage_k[p, ROWS : 2 * ROWS] = v_in[:, cols]
    kbuf[0, 0] = stage_k[me]
    for load in loads[2:]:
        load.wait()
    for p in range(GROUP):
        cols = slice(p * PAIR, (p + 1) * PAIR)
        stage_q[p, 0:ROWS] = q_in[:, cols]
        stage_q[p, ROWS : 2 * ROWS] = g_in[:, cols]

    product = g_in[...].astype(F32) * o_in[...].astype(F32)
    product = jnp.concatenate([product, product], axis=0)
    sums = jnp.concatenate([sums_in[...], sums_in[...]], axis=1)
    count = 16 * GROUP

    def row_of(shape):
        return lax.broadcasted_iota(jnp.int32, shape, 0)

    def col_of(shape):
        return lax.broadcasted_iota(jnp.int32, shape, 1)

    def pick(width, first, per_head):
        row, col = row_of((count, width)), col_of((count, width))
        kind = row % 4
        head = 2 * (row // 16) + kind - first
        hit = (row % 16 < 12) & (kind >= first) & (kind < first + 2) & (col // per_head == head)
        return jnp.where(hit, 1.0, 0.0).astype(BF)

    value = select_rows(dot_nt, pick(GROUP * PAIR, 2, HEAD), product)
    value += select_rows(dot_nn, pick(16, 0, 1), sums)
    high = value.astype(BF).astype(F32)
    mid = (value - high).astype(BF).astype(F32)
    low = value - high - mid
    row, col = row_of((count, PAIR)), col_of((count, PAIR))
    third = (row % 16) // 4
    value = jnp.where(third == 0, high, jnp.where(third == 1, mid, low))
    value = jnp.where(col // ROWS == (row // 16 + me) % 2, value, 0.0).astype(BF)
    for p in range(GROUP):
        stage_q[p, 2 * ROWS : SIDE] = value[16 * p : 16 * (p + 1)]

    qbuf[0, 0] = stage_q[me]

    pl.semaphore_wait(barrier, 19)
    for offset, other in near:
        near_copy(1, offset, other).start()
        near_copy(0, offset, other).start()
    for offset in (1, -1):
        for other in (0, 1):
            cross_copy(1, offset, other).start()
            cross_copy(0, offset, other).start()
    dq_acc[...] = jnp.zeros_like(dq_acc)
    dk_acc[...] = jnp.zeros_like(dk_acc)
    dv_acc[...] = jnp.zeros_like(dv_acc)

    lane = lax.broadcasted_iota(jnp.int32, (1, PAIR), 1)

    def prepare_q(slot):
        q = qbuf[slot, :, 0:ROWS, :].reshape(CHUNK, PAIR)
        g = qbuf[slot, :, ROWS : 2 * ROWS, :].reshape(CHUNK, PAIR)
        for h in range(2):
            own = jnp.where(lane // HEAD == h, 1.0, 0.0)
            qm[slot, h] = q * (own * HEAD**-0.5).astype(BF)
            gm[slot, h] = g * own.astype(BF)
        for i in range(RING):
            part = qbuf[slot, 2 * i, 2 * ROWS : SIDE, :].astype(F32)
            part += qbuf[slot, 2 * i + 1, 2 * ROWS : SIDE, :].astype(F32)
            terms[slot, 0:4, i * PAIR : (i + 1) * PAIR] = part[0:4] + part[4:8] + part[8:12]

    def prepare_k(slot):
        k = kbuf[slot, :, 0:ROWS, :].reshape(CHUNK, PAIR).astype(F32)
        kt[slot] = (k * HEAD**-0.5).T.astype(BF)

    def pass_on(chunk):
        for side in (1, 0):
            cross_all(side, chunk).wait_recv()
            for offset in OFFSETS[1:]:
                ring_copy(side, chunk, offset).start()

    def arrive(side, chunk):
        (near_all(side) if chunk == 0 else ring_all(side, chunk)).wait_recv()
        (prepare_q, prepare_k)[side](chunk)

    pass_on(1)
    for other in (0, 1):
        cross_copy(1, 2, other).start()
        cross_copy(0, 2, other).start()
    arrive(1, 0)
    arrive(0, 0)

    def tile(kslot, qslot):
        k = kbuf[kslot, :, 0:ROWS, :].reshape(CHUNK, PAIR)
        v = kbuf[kslot, :, ROWS : 2 * ROWS, :].reshape(CHUNK, PAIR)
        for h in range(2):
            q = qm[qslot, h]
            g = gm[qslot, h]
            probs = jnp.exp(dot_nt(k, q) - terms[qslot, h : h + 1, :])
            grad = probs * (dot_nt(v, g) - terms[qslot, 2 + h : 3 + h, :])
            grad = grad.astype(BF)
            dv_acc[kslot] += dot_nn(probs.astype(BF), g)
            dk_acc[kslot] += dot_nn(grad, q)
            rows = slice(h * HEAD, (h + 1) * HEAD)
            dq_acc[qslot, rows, :] += dot_nn(kt[kslot, rows, :], grad)

    half = 2 * ROWS

    def send_sums(chunk):
        for slot in FAR:
            rows = slice(slot * half, (slot + 1) * half)
            ring_kv[chunk, slot, 0] = dk_acc[chunk, rows].astype(BF)
            ring_kv[chunk, slot, 1] = dv_acc[chunk, rows].astype(BF)
        for offset in OFFSETS[1:]:
            sum_copy(chunk, offset).start()

    def hop(chunk):
        sum_all(chunk).wait_recv()
        for i, acc in enumerate((dk_acc, dv_acc)):
            total = acc[chunk, 0:half]
            for slot in FAR:
                total = total + came_kv[chunk, slot, i].astype(F32)
            for other in (0, 1):
                rows = slice(other * ROWS, (other + 1) * ROWS)
                back_kv[2 * chunk + other, i] = total[rows].astype(BF)
        for other in (0, 1):
            back_copy(chunk, other).start()

    def send_direct():
        for piece in range(1, GROUP):
            rows = slice(piece * ROWS, (piece + 1) * ROWS)
            near_kv[piece, 0] = dk_acc[0, rows].astype(BF)
            near_kv[piece, 1] = dv_acc[0, rows].astype(BF)
        for offset, other in near:
            direct_copy(offset, other).start()

    def send_query(chunk):
        total = dq_acc[chunk].T
        if not chunk:
            own_q[...] = total[0:ROWS]
        send_q[chunk] = total.astype(BF).reshape(GROUP, ROWS, PAIR)
        for offset, other in near + [(0, 0)] * bool(chunk):
            query_copy(chunk, offset, other).start()

    events = {}
    for chunk, i in FORWARD_AT.items():
        events.setdefault(i, []).append((pass_on, (chunk,)))
    seen = {(0, 0), (1, 0)}
    left = {(side, chunk): RING for side in range(2) for chunk in range(RING)}
    for i, order in enumerate(TILES):
        for side in (1, 0):
            chunk = order[1 - side]
            if (side, chunk) not in seen:
                seen.add((side, chunk))
                events.setdefault(i, []).append((arrive, (side, chunk)))
            left[side, chunk] -= 1
            if not left[side, chunk]:
                if not side:
                    events.setdefault(i + 1, []).append((send_query, (chunk,)))
                elif chunk:
                    events.setdefault(i + 1, []).append((send_sums, (chunk,)))
                    after = min(i + 1 + HOP_AFTER, STEPS + 1)
                    events.setdefault(after, []).append((hop, (chunk,)))
                else:
                    events.setdefault(i + 1, []).append((send_direct, ()))

    def run(i):
        for act, operands in events.get(i, []):
            act(*operands)

    for i, order in enumerate(TILES):
        run(i)
        tile(*order)
    run(STEPS)
    run(STEPS + 1)

    def columns(offset, other):
        return pl.ds(pl.multiple_of(pair_at(offset, other) * PAIR, PAIR), PAIR)

    def own_sum(first, parts):
        for part in parts:
            first = first + part.astype(F32)
        return first.astype(BF)

    back_all().wait_recv()
    for chunk in FAR:
        for other in (0, 1):
            cols = columns(-OFFSETS[chunk], other)
            piece = 2 * chunk + other
            out_ref[1, :, cols] = home_kv[piece, 0]
            out_ref[2, :, cols] = home_kv[piece, 1]
    for chunk in range(RING):
        query_all(chunk).wait_recv()
        for other in (0, 1):
            parts = [came_q[chunk, 2 * slot + other] for slot in range(RING)]
            first = parts[0].astype(F32) if chunk or other else own_q[...]
            out_ref[0, :, columns(-OFFSETS[chunk], other)] = own_sum(first, parts[1:])
    direct_all().wait_recv()
    for i, acc in enumerate((dk_acc, dv_acc)):
        for other in (0, 1):
            parts = [direct_kv[2 * slot + other, i] for slot in range(RING)]
            first = parts[0].astype(F32) if other else acc[0, 0:ROWS]
            out_ref[1 + i, :, columns(0, other)] = own_sum(first, parts[1:])

    back_all().wait_send()
    direct_all().wait_send()
    for chunk in range(RING):
        query_all(chunk).wait_send()
    for chunk in FAR:
        sum_all(chunk).wait_send()
    for side in range(2):
        near_all(side).wait_send()
        for chunk in FAR:
            cross_all(side, chunk).wait_send()
            ring_all(side, chunk).wait_send()


def shards(queries, key_rows, value_rows, output_rows, grad_out, log_sums):
    vmem = pl.BlockSpec(memory_space=pltpu.VMEM)
    hbm = pl.BlockSpec(memory_space=pltpu.HBM)
    out = jax.ShapeDtypeStruct((ROWS, GROUP * PAIR), F32)
    dma = pltpu.SemaphoreType.DMA
    arrays = (queries, key_rows, value_rows, output_rows, grad_out, log_sums.T)
    r = pl.pallas_call(
        kernel,
        out_shape=jax.ShapeDtypeStruct((3, ROWS, GROUP * PAIR), BF),
        in_specs=[hbm] * 6,
        out_specs=vmem,
        scratch_shapes=[pltpu.VMEM((ROWS, GROUP * PAIR), BF)] * 5 + [
            pltpu.VMEM((2 * GROUP, ROWS), F32),
            dma((6,)),
            pltpu.VMEM((GROUP, SIDE, PAIR), BF),
            pltpu.VMEM((GROUP, 2 * ROWS, PAIR), BF),
            pltpu.VMEM((RING, GROUP, SIDE, PAIR), BF),
            pltpu.VMEM((RING, GROUP, 2 * ROWS, PAIR), BF),
            pltpu.VMEM((RING, 2, CHUNK, PAIR), BF),
            pltpu.VMEM((RING, 2, CHUNK, PAIR), BF),
            pltpu.VMEM((RING, PAIR, CHUNK), BF),
            pltpu.VMEM((RING, 8, CHUNK), F32),
            pltpu.VMEM((RING, PAIR, CHUNK), F32),
            pltpu.VMEM((RING, CHUNK, PAIR), F32),
            pltpu.VMEM((RING, CHUNK, PAIR), F32),
            pltpu.VMEM((RING, RING, 2, 2 * ROWS, PAIR), BF),
            pltpu.VMEM((RING, RING, 2, 2 * ROWS, PAIR), BF),
            pltpu.VMEM((GROUP, 2, ROWS, PAIR), BF),
            pltpu.VMEM((GROUP, 2, ROWS, PAIR), BF),
            pltpu.VMEM((GROUP, 2, ROWS, PAIR), BF),
            pltpu.VMEM((GROUP, 2, ROWS, PAIR), BF),
            pltpu.VMEM((RING, GROUP, ROWS, PAIR), BF),
            pltpu.VMEM((RING, GROUP, ROWS, PAIR), BF),
            pltpu.VMEM((ROWS, PAIR), F32),
            dma((2, 2)),
            dma((2, 2, RING)),
            dma((2, 2, RING)),
            dma((2, RING)),
            dma((2,)),
            dma((2,)),
            dma((2, RING)),
        ],
        compiler_params=pltpu.CompilerParams(
            collective_id=0, has_side_effects=True, vmem_limit_bytes=48 * 2**20
        ),
        cost_estimate=pl.CostEstimate(
            flops=5 * 2**30, bytes_accessed=2**21, transcendentals=2**23
        ),
    )(*(pltpu.with_memory_space_constraint(array, pltpu.HBM) for array in arrays))
    return r[0].astype(F32), r[1].astype(F32), r[2].astype(F32)


def solution(mesh):
    q_side = P(("pb", "ka"), None)
    k_side = P(("ka", "pb"), None)
    return jax.shard_map(
        shards,
        mesh=mesh,
        in_specs=(q_side, k_side, k_side, q_side, q_side, q_side),
        out_specs=(q_side, k_side, k_side),
        check_vma=False,
    )
```

```python
import jax
import jax.numpy as jnp
from jax import lax
from jax.experimental import pallas as pl
from jax.experimental.pallas import tpu as pltpu
from jax.sharding import PartitionSpec as P

BF = jnp.bfloat16
F32 = jnp.float32
MESH = pl.DeviceIdType.MESH

ROWS = 64
PAIR = 128
HEAD = 64
GROUP = 8
RING = 4
CHUNK = 2 * RING * ROWS
SIDE = 2 * ROWS + 16
OFFSETS = (0, 1, -1, 2)
SLOT_AT = {1: 2, -1: 1, 2: 3}
FAR = (1, 2, 3)
WHOLE = (0, CHUNK)
NEAR = (0, 2 * ROWS)
REST = (2 * ROWS, CHUNK)


def dot_nn(a, b):
    return jnp.dot(a, b, preferred_element_type=F32)


def dot_nt(a, b):
    return lax.dot_general(a, b, (((1,), (1,)), ((), ())), preferred_element_type=F32)


def split3(value):
    high = value.astype(BF)
    rest = value - high.astype(F32)
    mid = rest.astype(BF)
    low = (rest - mid.astype(F32)).astype(BF)
    return high, mid, low


def select_rows(dot, matrix, value):
    high, mid, low = split3(value)
    return dot(matrix, high) + dot(matrix, mid) + dot(matrix, low)


def kernel(
    q_hbm, k_hbm, v_hbm, o_hbm, g_hbm, sums_hbm,
    out_ref,
    q_in, k_in, v_in, o_in, g_in, sums_in, load_sem,
    stage_q, stage_k, qbuf, kbuf, qm, gm, kt, terms,
    dq_acc, dk_acc, dv_acc,
    ring_kv, came_kv, back_kv, home_kv, near_kv, direct_kv, send_q, came_q, own_q,
    near_sem, cross_sem, ring_sem, sum_sem, back_sem, direct_sem, query_sem,
):
    loads = [
        pltpu.make_async_copy(src, dst, load_sem.at[i])
        for i, (src, dst) in enumerate((
            (k_hbm, k_in), (v_hbm, v_in), (g_hbm, g_in), (o_hbm, o_in), (sums_hbm, sums_in),
            (q_hbm, q_in),
        ))
    ]
    for load in loads:
        load.start()

    pb = lax.axis_index("pb")
    ka = lax.axis_index("ka")
    y = lax.rem(pb, 4)
    z_hi = pb // 4
    me = lax.rem(ka, 8)
    z_lo = ka // 8
    z = z_hi * 2 + z_lo

    x = me // 2
    core = lax.rem(me, 2)

    pairs = {
        (offset, other): lax.rem(x + (offset + 4), 4) * 2 + (1 - core if other else core)
        for offset in OFFSETS
        for other in (0, 1)
    }
    places = {}
    for offset in OFFSETS:
        at_y = lax.rem(y + (offset + 4), 4)
        at_z = lax.rem(z + (offset + 4), 4)
        for other in (0, 1):
            mine = z_lo * 8 + pairs[0, other]
            places["x", offset, other] = (pb, z_lo * 8 + pairs[offset, other])
            places["y", offset, other] = (z_hi * 4 + at_y, mine)
            for chunk in FAR:
                places["xy", chunk, offset, other] = (
                    z_hi * 4 + at_y, z_lo * 8 + pairs[OFFSETS[chunk], other]
                )
            places["z", offset, other] = (
                (at_z // 2) * 4 + y, lax.rem(at_z, 2) * 8 + pairs[0, other]
            )

    def pair_at(offset, other):
        return pairs[2 if offset == -2 else offset, other]

    def along_x(offset, other):
        return places["x", offset, other]

    def along_y(offset, other=0):
        return places["y", offset, other]

    def along_z(offset, other=0):
        return places["z", offset, other]

    rings = (along_y, along_z)

    barrier = pltpu.get_barrier_semaphore()
    for peer in [along_x(0, 1)] + [
        along(offset, other)
        for along in (along_x, along_y, along_z)
        for offset in OFFSETS[1:]
        for other in (0, 1)
    ]:
        pl.semaphore_signal(barrier, inc=1, device_id=peer, device_id_type=MESH)

    def remote(src, dst, sem, index, peer):
        return pltpu.make_async_remote_copy(
            src_ref=src, dst_ref=dst, send_sem=sem.at[(0, *index)], recv_sem=sem.at[(1, *index)],
            device_id=peer, device_id_type=MESH,
        )

    stages, bufs = (stage_q, stage_k), (qbuf, kbuf)
    others = slice(1, 8)
    afar = slice(2, 8)

    def near_copy(side, offset, other):
        piece = 2 * SLOT_AT.get(offset, 0) + other
        return remote(
            stages[side].at[pair_at(0, other)], bufs[side].at[0, piece],
            near_sem, (side,), rings[side](offset, other),
        )

    def near_all(side):
        view = bufs[side].at[0, others]
        return remote(view, view, near_sem, (side,), along_x(0, 1))

    def cross_copy(side, offset, other):
        chunk = SLOT_AT[offset]
        return remote(
            stages[side].at[pair_at(offset, other)], bufs[side].at[chunk, other],
            cross_sem, (side, chunk), along_x(offset, other),
        )

    def cross_all(side, chunk):
        view = bufs[side].at[chunk, 0:2]
        return remote(view, view, cross_sem, (side, chunk), along_x(0, 1))

    def ring_copy(side, chunk, offset):
        first = 2 * SLOT_AT[offset]
        return remote(
            bufs[side].at[chunk, 0:2], bufs[side].at[chunk, first : first + 2],
            ring_sem, (side, chunk), rings[side](offset),
        )

    def ring_all(side, chunk):
        view = bufs[side].at[chunk, afar]
        return remote(view, view, ring_sem, (side, chunk), along_x(0, 1))

    def sum_copy(chunk, offset):
        return remote(
            ring_kv.at[chunk, OFFSETS.index(offset)], came_kv.at[chunk, SLOT_AT[offset]],
            sum_sem, (chunk,), along_z(offset),
        )

    def sum_all(chunk):
        view = came_kv.at[chunk, 1:4]
        return remote(view, view, sum_sem, (chunk,), along_x(0, 1))

    def back_copy(chunk, other):
        piece = 2 * chunk + other
        return remote(
            back_kv.at[piece], home_kv.at[piece],
            back_sem, (), along_x(OFFSETS[chunk], other),
        )

    def back_all():
        view = home_kv.at[afar]
        return remote(view, view, back_sem, (), along_x(0, 1))

    def direct_copy(offset, other):
        return remote(
            near_kv.at[2 * OFFSETS.index(offset) + other],
            direct_kv.at[2 * SLOT_AT.get(offset, 0) + other],
            direct_sem, (), along_z(offset, other),
        )

    def direct_all():
        view = direct_kv.at[others]
        return remote(view, view, direct_sem, (), along_x(0, 1))

    def query_copy(chunk, offset, other):
        peer = places["xy", chunk, offset, other] if chunk else along_y(offset, other)
        return remote(
            send_q.at[chunk, 2 * OFFSETS.index(offset) + other],
            came_q.at[chunk, 2 * SLOT_AT.get(offset, 0) + other],
            query_sem, (chunk,), peer,
        )

    def query_all(chunk):
        view = came_q.at[chunk] if chunk else came_q.at[0, others]
        return remote(view, view, query_sem, (chunk,), along_x(0, 1))

    near = [(offset, other) for offset in (2, 1, -1, 0) for other in (0, 1)][:-2] + [(0, 1)]

    loads[0].wait()
    loads[1].wait()
    for p in range(GROUP):
        cols = slice(p * PAIR, (p + 1) * PAIR)
        stage_k[p, 0:ROWS] = k_in[:, cols]
        stage_k[p, ROWS : 2 * ROWS] = v_in[:, cols]
    kbuf[0, 0] = stage_k[me]
    for load in loads[2:]:
        load.wait()
    for p in range(GROUP):
        cols = slice(p * PAIR, (p + 1) * PAIR)
        stage_q[p, 0:ROWS] = q_in[:, cols]
        stage_q[p, ROWS : 2 * ROWS] = g_in[:, cols]

    product = g_in[...].astype(F32) * o_in[...].astype(F32)
    product = jnp.concatenate([product, product], axis=0)
    sums = jnp.concatenate([sums_in[...], sums_in[...]], axis=1)
    count = 16 * GROUP

    def row_of(shape):
        return lax.broadcasted_iota(jnp.int32, shape, 0)

    def col_of(shape):
        return lax.broadcasted_iota(jnp.int32, shape, 1)

    def pick(width, first, per_head):
        row, col = row_of((count, width)), col_of((count, width))
        kind = row % 4
        head = 2 * (row // 16) + kind - first
        hit = (row % 16 < 12) & (kind >= first) & (kind < first + 2) & (col // per_head == head)
        return jnp.where(hit, 1.0, 0.0).astype(BF)

    value = select_rows(dot_nt, pick(GROUP * PAIR, 2, HEAD), product)
    value += select_rows(dot_nn, pick(16, 0, 1), sums)
    high = value.astype(BF).astype(F32)
    mid = (value - high).astype(BF).astype(F32)
    low = value - high - mid
    row, col = row_of((count, PAIR)), col_of((count, PAIR))
    third = (row % 16) // 4
    value = jnp.where(third == 0, high, jnp.where(third == 1, mid, low))
    value = jnp.where(col // ROWS == (row // 16 + me) % 2, value, 0.0).astype(BF)
    for p in range(GROUP):
        stage_q[p, 2 * ROWS : SIDE] = value[16 * p : 16 * (p + 1)]

    qbuf[0, 0] = stage_q[me]

    pl.semaphore_wait(barrier, 19)
    for offset in (-1, 1):
        for other in (0, 1):
            cross_copy(1, offset, other).start()
            cross_copy(0, offset, other).start()
    for offset, other in near:
        near_copy(1, offset, other).start()
        near_copy(0, offset, other).start()
    dq_acc[...] = jnp.zeros_like(dq_acc)
    dk_acc[...] = jnp.zeros_like(dk_acc)
    dv_acc[...] = jnp.zeros_like(dv_acc)

    lane = lax.broadcasted_iota(jnp.int32, (1, PAIR), 1)

    def prepare_q(chunk, rows):
        first, last = rows
        pieces = slice(first // ROWS, last // ROWS)
        q = qbuf[chunk, pieces, 0:ROWS, :].reshape(last - first, PAIR)
        g = qbuf[chunk, pieces, ROWS : 2 * ROWS, :].reshape(last - first, PAIR)
        for h in range(2):
            own = jnp.where(lane // HEAD == h, 1.0, 0.0)
            qm[chunk, h, first:last] = q * (own * HEAD**-0.5).astype(BF)
            gm[chunk, h, first:last] = g * own.astype(BF)
        for i in range(first // PAIR, last // PAIR):
            part = qbuf[chunk, 2 * i, 2 * ROWS : SIDE, :].astype(F32)
            part += qbuf[chunk, 2 * i + 1, 2 * ROWS : SIDE, :].astype(F32)
            terms[chunk, 0:4, i * PAIR : (i + 1) * PAIR] = part[0:4] + part[4:8] + part[8:12]

    def keys(chunk, rows, low, high):
        first, last = rows
        pieces = slice(first // ROWS, last // ROWS)
        return kbuf[chunk, pieces, low:high, :].reshape(last - first, PAIR)

    def prepare_k(chunk, rows):
        k = keys(chunk, rows, 0, ROWS).astype(F32)
        kt[chunk, :, rows[0] : rows[1]] = (k * HEAD**-0.5).T.astype(BF)

    def pass_on(chunk):
        for side in (1, 0):
            cross_all(side, chunk).wait_recv()
            for offset in OFFSETS[1:]:
                ring_copy(side, chunk, offset).start()

    def arrive(side, chunk, rows=REST):
        (ring_all(side, chunk) if chunk else near_all(side)).wait_recv()
        (prepare_q, prepare_k)[side](chunk, rows)

    pass_on(1)
    for other in (0, 1):
        cross_copy(1, 2, other).start()
        cross_copy(0, 2, other).start()
    arrive(1, 0, WHOLE)
    arrive(0, 0, WHOLE)

    def join(parts, axis):
        return parts[0] if len(parts) == 1 else jnp.concatenate(parts, axis=axis)

    def tile(key_parts, query_parts):
        k = join([keys(chunk, rows, 0, ROWS) for chunk, rows in key_parts], 0)
        v = join([keys(chunk, rows, ROWS, 2 * ROWS) for chunk, rows in key_parts], 0)
        for h in range(2):
            head = slice(h * HEAD, (h + 1) * HEAD)
            q = join([qm[c, h, a:b] for c, (a, b) in query_parts], 0)
            g = join([gm[c, h, a:b] for c, (a, b) in query_parts], 0)
            sums = join([terms[c, h : h + 1, a:b] for c, (a, b) in query_parts], 1)
            delta = join([terms[c, 2 + h : 3 + h, a:b] for c, (a, b) in query_parts], 1)
            probs = jnp.exp(dot_nt(k, q) - sums)
            grad = (probs * (dot_nt(v, g) - delta)).astype(BF)
            dv = dot_nn(probs.astype(BF), g)
            dk = dot_nn(grad, q)
            dq = dot_nn(join([kt[c, head, a:b] for c, (a, b) in key_parts], 1), grad)
            at = 0
            for c, (a, b) in key_parts:
                dv_acc[c, a:b] += dv[at : at + b - a]
                dk_acc[c, a:b] += dk[at : at + b - a]
                at += b - a
            at = 0
            for c, (a, b) in query_parts:
                dq_acc[c, head, a:b] += dq[:, at : at + b - a]
                at += b - a

    def whole(kslot, qslot):
        tile([(kslot, WHOLE)], [(qslot, WHOLE)])

    half = 2 * ROWS

    def send_sums(chunk):
        for slot in FAR:
            rows = slice(slot * half, (slot + 1) * half)
            ring_kv[chunk, slot, 0] = dk_acc[chunk, rows].astype(BF)
            ring_kv[chunk, slot, 1] = dv_acc[chunk, rows].astype(BF)
        for offset in OFFSETS[1:]:
            sum_copy(chunk, offset).start()

    def hop(chunk):
        sum_all(chunk).wait_recv()
        for i, acc in enumerate((dk_acc, dv_acc)):
            total = acc[chunk, 0:half]
            for slot in FAR:
                total = total + came_kv[chunk, slot, i].astype(F32)
            for other in (0, 1):
                rows = slice(other * ROWS, (other + 1) * ROWS)
                back_kv[2 * chunk + other, i] = total[rows].astype(BF)
        for other in (0, 1):
            back_copy(chunk, other).start()

    def send_direct(pieces):
        for piece in pieces:
            rows = slice(piece * ROWS, (piece + 1) * ROWS)
            near_kv[piece, 0] = dk_acc[0, rows].astype(BF)
            near_kv[piece, 1] = dv_acc[0, rows].astype(BF)
        for piece in reversed(pieces):
            direct_copy(OFFSETS[piece // 2], piece % 2).start()

    def send_query(chunk, pieces):
        first, last = pieces[0] * ROWS, (pieces[-1] + 1) * ROWS
        total = dq_acc[chunk, :, first:last].T
        if chunk == 0:
            own_q[...] = total[0:ROWS]
        total = total.astype(BF).reshape(len(pieces), ROWS, PAIR)
        send_q[chunk, pieces[0] : pieces[-1] + 1] = total
        for piece in reversed(pieces):
            if chunk or piece:
                query_copy(chunk, OFFSETS[piece // 2], piece % 2).start()

    whole(0, 0)
    pass_on(2)
    for chunk in (1, 2):
        prepare_k(chunk, NEAR)
        prepare_q(chunk, NEAR)
    tile([(1, NEAR), (2, NEAR)], [(0, WHOLE)])
    arrive(1, 1)
    tile([(1, REST)], [(0, WHOLE)])
    pass_on(3)
    arrive(0, 1)
    whole(1, 1)
    arrive(1, 2)
    tile([(2, REST)], [(0, WHOLE)])
    whole(2, 1)
    arrive(0, 2)
    whole(2, 2)
    whole(1, 2)
    arrive(0, 3, WHOLE)
    whole(1, 3)
    send_sums(1)
    whole(2, 3)
    send_sums(2)
    whole(0, 3)
    arrive(1, 3, WHOLE)
    whole(3, 3)
    send_query(3, range(8))
    whole(3, 0)
    send_query(0, range(8))
    whole(3, 1)
    whole(3, 2)
    send_sums(3)
    hop(1)
    whole(0, 1)
    send_query(1, range(8))
    hop(2)
    whole(0, 2)
    send_direct(range(1, 8))
    send_query(2, range(8))
    hop(3)

    def columns(offset, other):
        return pl.ds(pl.multiple_of(pair_at(offset, other) * PAIR, PAIR), PAIR)

    def own_sum(first, parts):
        for part in parts:
            first = first + part.astype(F32)
        return first.astype(BF)

    for side in range(2):
        near_all(side).wait_send()
        for chunk in FAR:
            cross_all(side, chunk).wait_send()
            ring_all(side, chunk).wait_send()
    for chunk in (0, 1, 3):
        query_all(chunk).wait_send()
    for chunk in FAR:
        sum_all(chunk).wait_send()
    back_all().wait_send()

    back_all().wait_recv()
    for chunk in FAR:
        for other in (0, 1):
            cols = columns(-OFFSETS[chunk], other)
            piece = 2 * chunk + other
            out_ref[1, :, cols] = home_kv[piece, 0]
            out_ref[2, :, cols] = home_kv[piece, 1]
    for chunk in range(RING):
        query_all(chunk).wait_recv()
        for other in (0, 1):
            parts = [came_q[chunk, 2 * slot + other] for slot in range(RING)]
            first = parts[0].astype(F32) if chunk or other else own_q[...]
            out_ref[0, :, columns(-OFFSETS[chunk], other)] = own_sum(first, parts[1:])
    direct_all().wait_recv()
    for i, acc in enumerate((dk_acc, dv_acc)):
        for other in (0, 1):
            parts = [direct_kv[2 * slot + other, i] for slot in range(RING)]
            first = parts[0].astype(F32) if other else acc[0, 0:ROWS]
            out_ref[1 + i, :, columns(0, other)] = own_sum(first, parts[1:])
    direct_all().wait_send()
    query_all(2).wait_send()


def shards(queries, key_rows, value_rows, output_rows, grad_out, log_sums):
    vmem = pl.BlockSpec(memory_space=pltpu.VMEM)
    hbm = pl.BlockSpec(memory_space=pltpu.HBM)
    out = jax.ShapeDtypeStruct((ROWS, GROUP * PAIR), F32)
    dma = pltpu.SemaphoreType.DMA
    arrays = (queries, key_rows, value_rows, output_rows, grad_out, log_sums.T)
    r = pl.pallas_call(
        kernel,
        out_shape=jax.ShapeDtypeStruct((3, ROWS, GROUP * PAIR), BF),
        in_specs=[hbm] * 6,
        out_specs=vmem,
        scratch_shapes=[pltpu.VMEM((ROWS, GROUP * PAIR), BF)] * 5 + [
            pltpu.VMEM((2 * GROUP, ROWS), F32),
            dma((6,)),
            pltpu.VMEM((GROUP, SIDE, PAIR), BF),
            pltpu.VMEM((GROUP, 2 * ROWS, PAIR), BF),
            pltpu.VMEM((RING, GROUP, SIDE, PAIR), BF),
            pltpu.VMEM((RING, GROUP, 2 * ROWS, PAIR), BF),
            pltpu.VMEM((RING, 2, CHUNK, PAIR), BF),
            pltpu.VMEM((RING, 2, CHUNK, PAIR), BF),
            pltpu.VMEM((RING, PAIR, CHUNK), BF),
            pltpu.VMEM((RING, 8, CHUNK), F32),
            pltpu.VMEM((RING, PAIR, CHUNK), F32),
            pltpu.VMEM((RING, CHUNK, PAIR), F32),
            pltpu.VMEM((RING, CHUNK, PAIR), F32),
            pltpu.VMEM((RING, RING, 2, 2 * ROWS, PAIR), BF),
            pltpu.VMEM((RING, RING, 2, 2 * ROWS, PAIR), BF),
            pltpu.VMEM((GROUP, 2, ROWS, PAIR), BF),
            pltpu.VMEM((GROUP, 2, ROWS, PAIR), BF),
            pltpu.VMEM((GROUP, 2, ROWS, PAIR), BF),
            pltpu.VMEM((GROUP, 2, ROWS, PAIR), BF),
            pltpu.VMEM((RING, GROUP, ROWS, PAIR), BF),
            pltpu.VMEM((RING, GROUP, ROWS, PAIR), BF),
            pltpu.VMEM((ROWS, PAIR), F32),
            dma((2, 2)),
            dma((2, 2, RING)),
            dma((2, 2, RING)),
            dma((2, RING)),
            dma((2,)),
            dma((2,)),
            dma((2, RING)),
        ],
        compiler_params=pltpu.CompilerParams(
            collective_id=0, has_side_effects=True, vmem_limit_bytes=48 * 2**20
        ),
        cost_estimate=pl.CostEstimate(
            flops=5 * 2**30, bytes_accessed=2**21, transcendentals=2**23
        ),
    )(*(pltpu.with_memory_space_constraint(array, pltpu.HBM) for array in arrays))
    return r[0].astype(F32), r[1].astype(F32), r[2].astype(F32)


def solution(mesh):
    q_side = P(("pb", "ka"), None)
    k_side = P(("ka", "pb"), None)
    return jax.shard_map(
        shards,
        mesh=mesh,
        in_specs=(q_side, k_side, k_side, q_side, q_side, q_side),
        out_specs=(q_side, k_side, k_side),
        check_vma=False,
    )
```

```python
import jax
import jax.numpy as jnp
from jax import lax
from jax.experimental import pallas as pl
from jax.experimental.pallas import tpu as pltpu
from jax.sharding import PartitionSpec as P

BF = jnp.bfloat16
F32 = jnp.float32
MESH = pl.DeviceIdType.MESH

ROWS = 64
PAIR = 128
HEAD = 64
GROUP = 8
RING = 4
CHUNK = 2 * RING * ROWS
SIDE = 2 * ROWS + 16
OFFSETS = (0, 1, -1, 2)
SLOT_AT = {1: 2, -1: 1, 2: 3}
FAR = (1, 2, 3)
WHOLE = (0, CHUNK)
NEAR = (0, 2 * ROWS)
REST = (2 * ROWS, CHUNK)


def dot_nn(a, b):
    return jnp.dot(a, b, preferred_element_type=F32)


def dot_nt(a, b):
    return lax.dot_general(a, b, (((1,), (1,)), ((), ())), preferred_element_type=F32)


def split3(value):
    high = value.astype(BF)
    rest = value - high.astype(F32)
    mid = rest.astype(BF)
    low = (rest - mid.astype(F32)).astype(BF)
    return high, mid, low


def select_rows(dot, matrix, value):
    high, mid, low = split3(value)
    return dot(matrix, high) + dot(matrix, mid) + dot(matrix, low)


def kernel(
    q_hbm, k_hbm, v_hbm, o_hbm, g_hbm, sums_hbm,
    out_ref,
    q_in, k_in, v_in, o_in, g_in, sums_in, load_sem,
    stage_q, stage_k, qbuf, kbuf, qm, gm, kt, terms,
    dq_acc, dk_acc, dv_acc,
    ring_kv, came_kv, back_kv, home_kv, near_kv, direct_kv, send_q, came_q, own_q,
    near_sem, cross_sem, ring_sem, sum_sem, back_sem, direct_sem, query_sem,
):
    loads = [
        pltpu.make_async_copy(src, dst, load_sem.at[i])
        for i, (src, dst) in enumerate((
            (k_hbm, k_in), (v_hbm, v_in), (g_hbm, g_in), (o_hbm, o_in), (sums_hbm, sums_in),
            (q_hbm, q_in),
        ))
    ]
    for load in loads:
        load.start()

    pb = lax.axis_index("pb")
    ka = lax.axis_index("ka")
    y = lax.rem(pb, 4)
    z_hi = pb // 4
    me = lax.rem(ka, 8)
    z_lo = ka // 8
    z = z_hi * 2 + z_lo

    x = me // 2
    core = lax.rem(me, 2)

    pairs = {
        (offset, other): lax.rem(x + (offset + 4), 4) * 2 + (1 - core if other else core)
        for offset in OFFSETS
        for other in (0, 1)
    }
    places = {}
    for offset in OFFSETS:
        at_y = lax.rem(y + (offset + 4), 4)
        at_z = lax.rem(z + (offset + 4), 4)
        for other in (0, 1):
            mine = z_lo * 8 + pairs[0, other]
            places["x", offset, other] = (pb, z_lo * 8 + pairs[offset, other])
            places["y", offset, other] = (z_hi * 4 + at_y, mine)
            for chunk in FAR:
                places["xy", chunk, offset, other] = (
                    z_hi * 4 + at_y, z_lo * 8 + pairs[OFFSETS[chunk], other]
                )
            places["z", offset, other] = (
                (at_z // 2) * 4 + y, lax.rem(at_z, 2) * 8 + pairs[0, other]
            )

    def pair_at(offset, other):
        return pairs[2 if offset == -2 else offset, other]

    def along_x(offset, other):
        return places["x", offset, other]

    def along_y(offset, other=0):
        return places["y", offset, other]

    def along_z(offset, other=0):
        return places["z", offset, other]

    rings = (along_y, along_z)

    barrier = pltpu.get_barrier_semaphore()
    for peer in [along_x(0, 1)] + [
        along(offset, other)
        for along in (along_x, along_y, along_z)
        for offset in OFFSETS[1:]
        for other in (0, 1)
    ]:
        pl.semaphore_signal(barrier, inc=1, device_id=peer, device_id_type=MESH)

    def remote(src, dst, sem, index, peer):
        return pltpu.make_async_remote_copy(
            src_ref=src, dst_ref=dst, send_sem=sem.at[(0, *index)], recv_sem=sem.at[(1, *index)],
            device_id=peer, device_id_type=MESH,
        )

    stages, bufs = (stage_q, stage_k), (qbuf, kbuf)
    others = slice(1, 8)
    afar = slice(2, 8)

    def near_copy(side, offset, other):
        piece = 2 * SLOT_AT.get(offset, 0) + other
        return remote(
            stages[side].at[pair_at(0, other)], bufs[side].at[0, piece],
            near_sem, (side,), rings[side](offset, other),
        )

    def near_all(side):
        view = bufs[side].at[0, others]
        return remote(view, view, near_sem, (side,), along_x(0, 1))

    def cross_copy(side, offset, other):
        chunk = SLOT_AT[offset]
        return remote(
            stages[side].at[pair_at(offset, other)], bufs[side].at[chunk, other],
            cross_sem, (side, chunk), along_x(offset, other),
        )

    def cross_all(side, chunk):
        view = bufs[side].at[chunk, 0:2]
        return remote(view, view, cross_sem, (side, chunk), along_x(0, 1))

    def ring_copy(side, chunk, offset):
        first = 2 * SLOT_AT[offset]
        return remote(
            bufs[side].at[chunk, 0:2], bufs[side].at[chunk, first : first + 2],
            ring_sem, (side, chunk), rings[side](offset),
        )

    def ring_all(side, chunk):
        view = bufs[side].at[chunk, afar]
        return remote(view, view, ring_sem, (side, chunk), along_x(0, 1))

    def sum_copy(chunk, offset, i):
        return remote(
            ring_kv.at[chunk, i, OFFSETS.index(offset)], came_kv.at[chunk, i, SLOT_AT[offset]],
            sum_sem, (chunk, i), along_z(offset),
        )

    def sum_all(chunk, i):
        view = came_kv.at[chunk, i, 1:4]
        return remote(view, view, sum_sem, (chunk, i), along_x(0, 1))

    def back_copy(chunk, other, i):
        piece = 2 * chunk + other
        return remote(
            back_kv.at[piece, i], home_kv.at[piece, i],
            back_sem, (), along_x(OFFSETS[chunk], other),
        )

    def back_all():
        view = home_kv.at[afar]
        return remote(view, view, back_sem, (), along_x(0, 1))

    def direct_copy(offset, other):
        return remote(
            near_kv.at[2 * OFFSETS.index(offset) + other],
            direct_kv.at[2 * SLOT_AT.get(offset, 0) + other],
            direct_sem, (), along_z(offset, other),
        )

    def direct_all():
        view = direct_kv.at[others]
        return remote(view, view, direct_sem, (), along_x(0, 1))

    def query_copy(chunk, offset, other):
        peer = places["xy", chunk, offset, other] if chunk else along_y(offset, other)
        return remote(
            send_q.at[chunk, 2 * OFFSETS.index(offset) + other],
            came_q.at[chunk, 2 * SLOT_AT.get(offset, 0) + other],
            query_sem, (chunk,), peer,
        )

    def query_all(chunk):
        view = came_q.at[chunk] if chunk else came_q.at[0, others]
        return remote(view, view, query_sem, (chunk,), along_x(0, 1))

    near = [(offset, other) for offset in (2, 1, -1, 0) for other in (0, 1)][:-2] + [(0, 1)]

    loads[0].wait()
    loads[1].wait()
    for p in range(GROUP):
        cols = slice(p * PAIR, (p + 1) * PAIR)
        stage_k[p, 0:ROWS] = k_in[:, cols]
        stage_k[p, ROWS : 2 * ROWS] = v_in[:, cols]
    kbuf[0, 0] = stage_k[me]
    for load in loads[2:]:
        load.wait()
    for p in range(GROUP):
        cols = slice(p * PAIR, (p + 1) * PAIR)
        stage_q[p, 0:ROWS] = q_in[:, cols]
        stage_q[p, ROWS : 2 * ROWS] = g_in[:, cols]

    product = g_in[...].astype(F32) * o_in[...].astype(F32)
    product = jnp.concatenate([product, product], axis=0)
    sums = jnp.concatenate([sums_in[...], sums_in[...]], axis=1)
    count = 16 * GROUP

    def row_of(shape):
        return lax.broadcasted_iota(jnp.int32, shape, 0)

    def col_of(shape):
        return lax.broadcasted_iota(jnp.int32, shape, 1)

    def pick(width, first, per_head):
        row, col = row_of((count, width)), col_of((count, width))
        kind = row % 4
        head = 2 * (row // 16) + kind - first
        hit = (row % 16 < 12) & (kind >= first) & (kind < first + 2) & (col // per_head == head)
        return jnp.where(hit, 1.0, 0.0).astype(BF)

    value = select_rows(dot_nt, pick(GROUP * PAIR, 2, HEAD), product)
    value += select_rows(dot_nn, pick(16, 0, 1), sums)
    high = value.astype(BF).astype(F32)
    mid = (value - high).astype(BF).astype(F32)
    low = value - high - mid
    row, col = row_of((count, PAIR)), col_of((count, PAIR))
    third = (row % 16) // 4
    value = jnp.where(third == 0, high, jnp.where(third == 1, mid, low))
    value = jnp.where(col // ROWS == (row // 16 + me) % 2, value, 0.0).astype(BF)
    for p in range(GROUP):
        stage_q[p, 2 * ROWS : SIDE] = value[16 * p : 16 * (p + 1)]

    qbuf[0, 0] = stage_q[me]

    pl.semaphore_wait(barrier, 19)
    for offset in (-1, 1):
        for other in (0, 1):
            cross_copy(1, offset, other).start()
            cross_copy(0, offset, other).start()
    for offset, other in near:
        near_copy(1, offset, other).start()
        near_copy(0, offset, other).start()
    dq_acc[...] = jnp.zeros_like(dq_acc)
    dk_acc[...] = jnp.zeros_like(dk_acc)
    dv_acc[...] = jnp.zeros_like(dv_acc)

    lane = lax.broadcasted_iota(jnp.int32, (1, PAIR), 1)

    def prepare_q(chunk, rows):
        first, last = rows
        pieces = slice(first // ROWS, last // ROWS)
        q = qbuf[chunk, pieces, 0:ROWS, :].reshape(last - first, PAIR)
        g = qbuf[chunk, pieces, ROWS : 2 * ROWS, :].reshape(last - first, PAIR)
        for h in range(2):
            own = jnp.where(lane // HEAD == h, 1.0, 0.0)
            qm[chunk, h, first:last] = q * (own * HEAD**-0.5).astype(BF)
            gm[chunk, h, first:last] = g * own.astype(BF)
        for i in range(first // PAIR, last // PAIR):
            part = qbuf[chunk, 2 * i, 2 * ROWS : SIDE, :].astype(F32)
            part += qbuf[chunk, 2 * i + 1, 2 * ROWS : SIDE, :].astype(F32)
            terms[chunk, 0:4, i * PAIR : (i + 1) * PAIR] = part[0:4] + part[4:8] + part[8:12]

    def keys(chunk, rows, low, high):
        first, last = rows
        pieces = slice(first // ROWS, last // ROWS)
        return kbuf[chunk, pieces, low:high, :].reshape(last - first, PAIR)

    def prepare_k(chunk, rows):
        k = keys(chunk, rows, 0, ROWS).astype(F32)
        kt[chunk, :, rows[0] : rows[1]] = (k * HEAD**-0.5).T.astype(BF)

    def pass_on(chunk):
        for side in (1, 0):
            cross_all(side, chunk).wait_recv()
            for offset in OFFSETS[1:]:
                ring_copy(side, chunk, offset).start()

    def arrive(side, chunk, rows=REST):
        (ring_all(side, chunk) if chunk else near_all(side)).wait_recv()
        (prepare_q, prepare_k)[side](chunk, rows)

    pass_on(1)
    for other in (0, 1):
        cross_copy(1, 2, other).start()
        cross_copy(0, 2, other).start()
    arrive(1, 0, WHOLE)
    arrive(0, 0, WHOLE)

    def join(parts, axis):
        return parts[0] if len(parts) == 1 else jnp.concatenate(parts, axis=axis)

    def tile(key_parts, query_parts):
        k = join([keys(chunk, rows, 0, ROWS) for chunk, rows in key_parts], 0)
        v = join([keys(chunk, rows, ROWS, 2 * ROWS) for chunk, rows in key_parts], 0)
        for h in range(2):
            head = slice(h * HEAD, (h + 1) * HEAD)
            q = join([qm[c, h, a:b] for c, (a, b) in query_parts], 0)
            g = join([gm[c, h, a:b] for c, (a, b) in query_parts], 0)
            sums = join([terms[c, h : h + 1, a:b] for c, (a, b) in query_parts], 1)
            delta = join([terms[c, 2 + h : 3 + h, a:b] for c, (a, b) in query_parts], 1)
            probs = jnp.exp(dot_nt(k, q) - sums)
            grad = (probs * (dot_nt(v, g) - delta)).astype(BF)
            dv = dot_nn(probs.astype(BF), g)
            dk = dot_nn(grad, q)
            dq = dot_nn(join([kt[c, head, a:b] for c, (a, b) in key_parts], 1), grad)
            at = 0
            for c, (a, b) in key_parts:
                dv_acc[c, a:b] += dv[at : at + b - a]
                dk_acc[c, a:b] += dk[at : at + b - a]
                at += b - a
            at = 0
            for c, (a, b) in query_parts:
                dq_acc[c, head, a:b] += dq[:, at : at + b - a]
                at += b - a

    def whole(kslot, qslot):
        tile([(kslot, WHOLE)], [(qslot, WHOLE)])

    half = 2 * ROWS

    def send_sums(chunk):
        for i, acc in enumerate((dk_acc, dv_acc)):
            for slot in FAR:
                rows = slice(slot * half, (slot + 1) * half)
                ring_kv[chunk, i, slot] = acc[chunk, rows].astype(BF)
            for offset in OFFSETS[1:]:
                sum_copy(chunk, offset, i).start()

    def hop(chunk):
        for i, acc in enumerate((dk_acc, dv_acc)):
            sum_all(chunk, i).wait_recv()
            total = acc[chunk, 0:half]
            for slot in FAR:
                total = total + came_kv[chunk, i, slot].astype(F32)
            for other in (0, 1):
                rows = slice(other * ROWS, (other + 1) * ROWS)
                back_kv[2 * chunk + other, i] = total[rows].astype(BF)
                back_copy(chunk, other, i).start()

    def send_direct(pieces):
        for piece in pieces:
            rows = slice(piece * ROWS, (piece + 1) * ROWS)
            near_kv[piece, 0] = dk_acc[0, rows].astype(BF)
            near_kv[piece, 1] = dv_acc[0, rows].astype(BF)
        for piece in reversed(pieces):
            direct_copy(OFFSETS[piece // 2], piece % 2).start()

    def send_query(chunk, pieces):
        first, last = pieces[0] * ROWS, (pieces[-1] + 1) * ROWS
        total = dq_acc[chunk, :, first:last].T
        if chunk == 0:
            own_q[...] = total[0:ROWS]
        total = total.astype(BF).reshape(len(pieces), ROWS, PAIR)
        send_q[chunk, pieces[0] : pieces[-1] + 1] = total
        for piece in reversed(pieces):
            if chunk or piece:
                query_copy(chunk, OFFSETS[piece // 2], piece % 2).start()

    whole(0, 0)
    pass_on(2)
    for chunk in (1, 2):
        prepare_k(chunk, NEAR)
        prepare_q(chunk, NEAR)
    tile([(1, NEAR), (2, NEAR)], [(0, WHOLE)])
    arrive(1, 1)
    tile([(1, REST)], [(0, WHOLE)])
    pass_on(3)
    arrive(0, 1)
    whole(1, 1)
    arrive(1, 2)
    tile([(2, REST)], [(0, WHOLE)])
    whole(2, 1)
    arrive(0, 2)
    whole(2, 2)
    whole(1, 2)
    arrive(0, 3, WHOLE)
    whole(1, 3)
    send_sums(1)
    whole(2, 3)
    send_sums(2)
    whole(0, 3)
    arrive(1, 3, WHOLE)
    whole(3, 3)
    send_query(3, range(8))
    whole(3, 0)
    send_query(0, range(8))
    whole(3, 1)
    whole(3, 2)
    send_sums(3)
    hop(1)
    whole(0, 1)
    send_query(1, range(8))
    hop(2)
    whole(0, 2)
    send_query(2, range(8))
    send_direct(range(1, 8))
    hop(3)

    def columns(offset, other):
        return pl.ds(pl.multiple_of(pair_at(offset, other) * PAIR, PAIR), PAIR)

    def own_sum(first, parts):
        for part in parts:
            first = first + part.astype(F32)
        return first.astype(BF)

    for side in range(2):
        near_all(side).wait_send()
        for chunk in FAR:
            cross_all(side, chunk).wait_send()
            ring_all(side, chunk).wait_send()
    for chunk in (0, 1, 3):
        query_all(chunk).wait_send()
    for chunk in FAR:
        for i in range(2):
            sum_all(chunk, i).wait_send()
    back_all().wait_send()

    back_all().wait_recv()
    for chunk in FAR:
        for other in (0, 1):
            cols = columns(-OFFSETS[chunk], other)
            piece = 2 * chunk + other
            out_ref[1, :, cols] = home_kv[piece, 0]
            out_ref[2, :, cols] = home_kv[piece, 1]
    for chunk in range(RING):
        query_all(chunk).wait_recv()
        for other in (0, 1):
            parts = [came_q[chunk, 2 * slot + other] for slot in range(RING)]
            first = parts[0].astype(F32) if chunk or other else own_q[...]
            out_ref[0, :, columns(-OFFSETS[chunk], other)] = own_sum(first, parts[1:])
    direct_all().wait_recv()
    for i, acc in enumerate((dk_acc, dv_acc)):
        for other in (0, 1):
            parts = [direct_kv[2 * slot + other, i] for slot in range(RING)]
            first = parts[0].astype(F32) if other else acc[0, 0:ROWS]
            out_ref[1 + i, :, columns(0, other)] = own_sum(first, parts[1:])
    direct_all().wait_send()
    query_all(2).wait_send()


def shards(queries, key_rows, value_rows, output_rows, grad_out, log_sums):
    vmem = pl.BlockSpec(memory_space=pltpu.VMEM)
    hbm = pl.BlockSpec(memory_space=pltpu.HBM)
    out = jax.ShapeDtypeStruct((ROWS, GROUP * PAIR), F32)
    dma = pltpu.SemaphoreType.DMA
    arrays = (queries, key_rows, value_rows, output_rows, grad_out, log_sums.T)
    r = pl.pallas_call(
        kernel,
        out_shape=jax.ShapeDtypeStruct((3, ROWS, GROUP * PAIR), BF),
        in_specs=[hbm] * 6,
        out_specs=vmem,
        scratch_shapes=[pltpu.VMEM((ROWS, GROUP * PAIR), BF)] * 5 + [
            pltpu.VMEM((2 * GROUP, ROWS), F32),
            dma((6,)),
            pltpu.VMEM((GROUP, SIDE, PAIR), BF),
            pltpu.VMEM((GROUP, 2 * ROWS, PAIR), BF),
            pltpu.VMEM((RING, GROUP, SIDE, PAIR), BF),
            pltpu.VMEM((RING, GROUP, 2 * ROWS, PAIR), BF),
            pltpu.VMEM((RING, 2, CHUNK, PAIR), BF),
            pltpu.VMEM((RING, 2, CHUNK, PAIR), BF),
            pltpu.VMEM((RING, PAIR, CHUNK), BF),
            pltpu.VMEM((RING, 8, CHUNK), F32),
            pltpu.VMEM((RING, PAIR, CHUNK), F32),
            pltpu.VMEM((RING, CHUNK, PAIR), F32),
            pltpu.VMEM((RING, CHUNK, PAIR), F32),
            pltpu.VMEM((RING, 2, RING, 2 * ROWS, PAIR), BF),
            pltpu.VMEM((RING, 2, RING, 2 * ROWS, PAIR), BF),
            pltpu.VMEM((GROUP, 2, ROWS, PAIR), BF),
            pltpu.VMEM((GROUP, 2, ROWS, PAIR), BF),
            pltpu.VMEM((GROUP, 2, ROWS, PAIR), BF),
            pltpu.VMEM((GROUP, 2, ROWS, PAIR), BF),
            pltpu.VMEM((RING, GROUP, ROWS, PAIR), BF),
            pltpu.VMEM((RING, GROUP, ROWS, PAIR), BF),
            pltpu.VMEM((ROWS, PAIR), F32),
            dma((2, 2)),
            dma((2, 2, RING)),
            dma((2, 2, RING)),
            dma((2, RING, 2)),
            dma((2,)),
            dma((2,)),
            dma((2, RING)),
        ],
        compiler_params=pltpu.CompilerParams(
            collective_id=0, has_side_effects=True, vmem_limit_bytes=48 * 2**20
        ),
        cost_estimate=pl.CostEstimate(
            flops=5 * 2**30, bytes_accessed=2**21, transcendentals=2**23
        ),
    )(*(pltpu.with_memory_space_constraint(array, pltpu.HBM) for array in arrays))
    return r[0].astype(F32), r[1].astype(F32), r[2].astype(F32)


def solution(mesh):
    q_side = P(("pb", "ka"), None)
    k_side = P(("ka", "pb"), None)
    return jax.shard_map(
        shards,
        mesh=mesh,
        in_specs=(q_side, k_side, k_side, q_side, q_side, q_side),
        out_specs=(q_side, k_side, k_side),
        check_vma=False,
    )
```

```python
import jax
import jax.numpy as jnp
from jax import lax
from jax.experimental import pallas as pl
from jax.experimental.pallas import tpu as pltpu
from jax.sharding import PartitionSpec as P

BF = jnp.bfloat16
F32 = jnp.float32
MESH = pl.DeviceIdType.MESH

ROWS = 64
PAIR = 128
HEAD = 64
GROUP = 8
RING = 4
CHUNK = 2 * RING * ROWS
SIDE = 2 * ROWS + 16
OFFSETS = (0, 1, -1, 2)
SLOT_AT = {1: 2, -1: 1, 2: 3}
FAR = (1, 2, 3)
WHOLE = (0, CHUNK)
NEAR = (0, 2 * ROWS)
REST = (2 * ROWS, CHUNK)


def dot_nn(a, b):
    return jnp.dot(a, b, preferred_element_type=F32)


def dot_nt(a, b):
    return lax.dot_general(a, b, (((1,), (1,)), ((), ())), preferred_element_type=F32)


def split3(value):
    high = value.astype(BF)
    rest = value - high.astype(F32)
    mid = rest.astype(BF)
    low = (rest - mid.astype(F32)).astype(BF)
    return high, mid, low


def select_rows(dot, matrix, value):
    high, mid, low = split3(value)
    return dot(matrix, high) + dot(matrix, mid) + dot(matrix, low)


def kernel(
    q_hbm, k_hbm, v_hbm, o_hbm, g_hbm, sums_hbm,
    out_ref,
    q_in, k_in, v_in, o_in, g_in, sums_in, load_sem,
    stage_q, stage_k, qbuf, kbuf, qm, gm, kt, terms,
    dq_acc, dk_acc, dv_acc,
    ring_kv, came_kv, back_kv, home_kv, near_kv, direct_kv, send_q, came_q, own_q,
    near_sem, cross_sem, ring_sem, sum_sem, back_sem, direct_sem, query_sem,
):
    loads = [
        pltpu.make_async_copy(src, dst, load_sem.at[i])
        for i, (src, dst) in enumerate((
            (k_hbm, k_in), (v_hbm, v_in), (g_hbm, g_in), (o_hbm, o_in), (sums_hbm, sums_in),
            (q_hbm, q_in),
        ))
    ]
    for load in loads:
        load.start()

    pb = lax.axis_index("pb")
    ka = lax.axis_index("ka")
    y = lax.rem(pb, 4)
    z_hi = pb // 4
    me = lax.rem(ka, 8)
    z_lo = ka // 8
    z = z_hi * 2 + z_lo

    x = me // 2
    core = lax.rem(me, 2)

    pairs = {
        (offset, other): lax.rem(x + (offset + 4), 4) * 2 + (1 - core if other else core)
        for offset in OFFSETS
        for other in (0, 1)
    }
    places = {}
    for offset in OFFSETS:
        at_y = lax.rem(y + (offset + 4), 4)
        at_z = lax.rem(z + (offset + 4), 4)
        for other in (0, 1):
            mine = z_lo * 8 + pairs[0, other]
            places["x", offset, other] = (pb, z_lo * 8 + pairs[offset, other])
            places["y", offset, other] = (z_hi * 4 + at_y, mine)
            for chunk in FAR:
                places["xy", chunk, offset, other] = (
                    z_hi * 4 + at_y, z_lo * 8 + pairs[OFFSETS[chunk], other]
                )
            places["z", offset, other] = (
                (at_z // 2) * 4 + y, lax.rem(at_z, 2) * 8 + pairs[0, other]
            )

    def pair_at(offset, other):
        return pairs[2 if offset == -2 else offset, other]

    def along_x(offset, other):
        return places["x", offset, other]

    def along_y(offset, other=0):
        return places["y", offset, other]

    def along_z(offset, other=0):
        return places["z", offset, other]

    rings = (along_y, along_z)

    barrier = pltpu.get_barrier_semaphore()
    for peer in [along_x(0, 1)] + [
        along(offset, other)
        for along in (along_x, along_y, along_z)
        for offset in OFFSETS[1:]
        for other in (0, 1)
        if (along, offset) != (along_x, 2)
    ]:
        pl.semaphore_signal(barrier, inc=1, device_id=peer, device_id_type=MESH)

    def remote(src, dst, sem, index, peer):
        return pltpu.make_async_remote_copy(
            src_ref=src, dst_ref=dst, send_sem=sem.at[(0, *index)], recv_sem=sem.at[(1, *index)],
            device_id=peer, device_id_type=MESH,
        )

    stages, bufs = (stage_q, stage_k), (qbuf, kbuf)
    others = slice(1, 8)
    afar = slice(2, 8)

    def near_copy(side, offset, other):
        piece = 2 * SLOT_AT.get(offset, 0) + other
        return remote(
            stages[side].at[pair_at(0, other)], bufs[side].at[0, piece],
            near_sem, (side,), rings[side](offset, other),
        )

    def near_all(side):
        view = bufs[side].at[0, others]
        return remote(view, view, near_sem, (side,), along_x(0, 1))

    def cross_copy(side, offset, other):
        chunk = SLOT_AT[offset]
        return remote(
            stages[side].at[pair_at(offset, other)], bufs[side].at[chunk, other],
            cross_sem, (side, chunk), along_x(offset, other),
        )

    def cross_all(side, chunk):
        view = bufs[side].at[chunk, 0:2]
        return remote(view, view, cross_sem, (side, chunk), along_x(0, 1))

    def ring_copy(side, chunk, offset):
        first = 2 * SLOT_AT[offset]
        return remote(
            bufs[side].at[chunk, 0:2], bufs[side].at[chunk, first : first + 2],
            ring_sem, (side, chunk), rings[side](offset),
        )

    def ring_all(side, chunk):
        view = bufs[side].at[chunk, afar]
        return remote(view, view, ring_sem, (side, chunk), along_x(0, 1))

    def sum_copy(chunk, offset, i):
        return remote(
            ring_kv.at[chunk, i, OFFSETS.index(offset)], came_kv.at[chunk, i, SLOT_AT[offset]],
            sum_sem, (chunk, i), along_z(offset),
        )

    def sum_all(chunk, i):
        view = came_kv.at[chunk, i, 1:4]
        return remote(view, view, sum_sem, (chunk, i), along_x(0, 1))

    def back_copy(chunk, other, i):
        piece = 2 * chunk + other
        return remote(
            back_kv.at[piece, i], home_kv.at[piece, i],
            back_sem, (), along_x(OFFSETS[chunk], other),
        )

    def back_all():
        view = home_kv.at[afar]
        return remote(view, view, back_sem, (), along_x(0, 1))

    def direct_copy(offset, other):
        return remote(
            near_kv.at[2 * OFFSETS.index(offset) + other],
            direct_kv.at[2 * SLOT_AT.get(offset, 0) + other],
            direct_sem, (), along_z(offset, other),
        )

    def direct_all():
        view = direct_kv.at[others]
        return remote(view, view, direct_sem, (), along_x(0, 1))

    def query_copy(chunk, offset, other):
        peer = places["xy", chunk, offset, other] if chunk else along_y(offset, other)
        return remote(
            send_q.at[chunk, 2 * OFFSETS.index(offset) + other],
            came_q.at[chunk, 2 * SLOT_AT.get(offset, 0) + other],
            query_sem, (chunk,), peer,
        )

    def query_all(chunk):
        view = came_q.at[chunk] if chunk else came_q.at[0, others]
        return remote(view, view, query_sem, (chunk,), along_x(0, 1))

    near = [(offset, other) for offset in (2, 1, -1, 0) for other in (0, 1)][:-2] + [(0, 1)]

    loads[0].wait()
    loads[1].wait()
    for p in range(GROUP):
        cols = slice(p * PAIR, (p + 1) * PAIR)
        stage_k[p, 0:ROWS] = k_in[:, cols]
        stage_k[p, ROWS : 2 * ROWS] = v_in[:, cols]
    kbuf[0, 0] = stage_k[me]
    for load in loads[2:]:
        load.wait()
    for p in range(GROUP):
        cols = slice(p * PAIR, (p + 1) * PAIR)
        stage_q[p, 0:ROWS] = q_in[:, cols]
        stage_q[p, ROWS : 2 * ROWS] = g_in[:, cols]

    product = g_in[...].astype(F32) * o_in[...].astype(F32)
    product = jnp.concatenate([product, product], axis=0)
    sums = jnp.concatenate([sums_in[...], sums_in[...]], axis=1)
    count = 16 * GROUP

    def row_of(shape):
        return lax.broadcasted_iota(jnp.int32, shape, 0)

    def col_of(shape):
        return lax.broadcasted_iota(jnp.int32, shape, 1)

    def pick(width, first, per_head):
        row, col = row_of((count, width)), col_of((count, width))
        kind = row % 4
        head = 2 * (row // 16) + kind - first
        hit = (row % 16 < 12) & (kind >= first) & (kind < first + 2) & (col // per_head == head)
        return jnp.where(hit, 1.0, 0.0).astype(BF)

    value = select_rows(dot_nt, pick(GROUP * PAIR, 2, HEAD), product)
    value += select_rows(dot_nn, pick(16, 0, 1), sums)
    high = value.astype(BF).astype(F32)
    mid = (value - high).astype(BF).astype(F32)
    low = value - high - mid
    row, col = row_of((count, PAIR)), col_of((count, PAIR))
    third = (row % 16) // 4
    value = jnp.where(third == 0, high, jnp.where(third == 1, mid, low))
    value = jnp.where(col // ROWS == (row // 16 + me) % 2, value, 0.0).astype(BF)
    for p in range(GROUP):
        stage_q[p, 2 * ROWS : SIDE] = value[16 * p : 16 * (p + 1)]

    qbuf[0, 0] = stage_q[me]

    pl.semaphore_wait(barrier, 17)
    for offset in (-1, 1):
        for other in (0, 1):
            cross_copy(1, offset, other).start()
            cross_copy(0, offset, other).start()
    for offset, other in near:
        near_copy(1, offset, other).start()
        near_copy(0, offset, other).start()
    dq_acc[...] = jnp.zeros_like(dq_acc)
    dk_acc[...] = jnp.zeros_like(dk_acc)
    dv_acc[...] = jnp.zeros_like(dv_acc)

    lane = lax.broadcasted_iota(jnp.int32, (1, PAIR), 1)

    def prepare_q(chunk, rows):
        first, last = rows
        pieces = slice(first // ROWS, last // ROWS)
        q = qbuf[chunk, pieces, 0:ROWS, :].reshape(last - first, PAIR)
        g = qbuf[chunk, pieces, ROWS : 2 * ROWS, :].reshape(last - first, PAIR)
        for h in range(2):
            own = jnp.where(lane // HEAD == h, 1.0, 0.0)
            qm[chunk, h, first:last] = q * (own * HEAD**-0.5).astype(BF)
            gm[chunk, h, first:last] = g * own.astype(BF)
        for i in range(first // PAIR, last // PAIR):
            part = qbuf[chunk, 2 * i, 2 * ROWS : SIDE, :].astype(F32)
            part += qbuf[chunk, 2 * i + 1, 2 * ROWS : SIDE, :].astype(F32)
            terms[chunk, 0:4, i * PAIR : (i + 1) * PAIR] = part[0:4] + part[4:8] + part[8:12]

    def keys(chunk, rows, low, high):
        first, last = rows
        pieces = slice(first // ROWS, last // ROWS)
        return kbuf[chunk, pieces, low:high, :].reshape(last - first, PAIR)

    def prepare_k(chunk, rows):
        k = keys(chunk, rows, 0, ROWS).astype(F32)
        kt[chunk, :, rows[0] : rows[1]] = (k * HEAD**-0.5).T.astype(BF)

    def pass_on(chunk):
        for side in (1, 0):
            cross_all(side, chunk).wait_recv()
            for offset in OFFSETS[1:]:
                ring_copy(side, chunk, offset).start()

    def arrive(side, chunk, rows=REST):
        (ring_all(side, chunk) if chunk else near_all(side)).wait_recv()
        (prepare_q, prepare_k)[side](chunk, rows)

    pass_on(1)
    for other in (0, 1):
        cross_copy(1, 2, other).start()
        cross_copy(0, 2, other).start()
    arrive(1, 0, WHOLE)
    arrive(0, 0, WHOLE)

    def join(parts, axis):
        return parts[0] if len(parts) == 1 else jnp.concatenate(parts, axis=axis)

    def tile(key_parts, query_parts):
        k = join([keys(chunk, rows, 0, ROWS) for chunk, rows in key_parts], 0)
        v = join([keys(chunk, rows, ROWS, 2 * ROWS) for chunk, rows in key_parts], 0)
        for h in range(2):
            head = slice(h * HEAD, (h + 1) * HEAD)
            q = join([qm[c, h, a:b] for c, (a, b) in query_parts], 0)
            g = join([gm[c, h, a:b] for c, (a, b) in query_parts], 0)
            sums = join([terms[c, h : h + 1, a:b] for c, (a, b) in query_parts], 1)
            delta = join([terms[c, 2 + h : 3 + h, a:b] for c, (a, b) in query_parts], 1)
            probs = jnp.exp(dot_nt(k, q) - sums)
            grad = (probs * (dot_nt(v, g) - delta)).astype(BF)
            dv = dot_nn(probs.astype(BF), g)
            dk = dot_nn(grad, q)
            dq = dot_nn(join([kt[c, head, a:b] for c, (a, b) in key_parts], 1), grad)
            at = 0
            for c, (a, b) in key_parts:
                dv_acc[c, a:b] += dv[at : at + b - a]
                dk_acc[c, a:b] += dk[at : at + b - a]
                at += b - a
            at = 0
            for c, (a, b) in query_parts:
                dq_acc[c, head, a:b] += dq[:, at : at + b - a]
                at += b - a

    def whole(kslot, qslot):
        tile([(kslot, WHOLE)], [(qslot, WHOLE)])

    half = 2 * ROWS

    def send_sums(chunk):
        for i, acc in enumerate((dk_acc, dv_acc)):
            for slot in FAR:
                rows = slice(slot * half, (slot + 1) * half)
                ring_kv[chunk, i, slot] = acc[chunk, rows].astype(BF)
            for offset in OFFSETS[1:]:
                sum_copy(chunk, offset, i).start()

    def hop(chunk):
        for i, acc in enumerate((dk_acc, dv_acc)):
            sum_all(chunk, i).wait_recv()
            total = acc[chunk, 0:half]
            for slot in FAR:
                total = total + came_kv[chunk, i, slot].astype(F32)
            for other in (0, 1):
                rows = slice(other * ROWS, (other + 1) * ROWS)
                back_kv[2 * chunk + other, i] = total[rows].astype(BF)
                back_copy(chunk, other, i).start()

    def send_direct(pieces):
        for piece in pieces:
            rows = slice(piece * ROWS, (piece + 1) * ROWS)
            near_kv[piece, 0] = dk_acc[0, rows].astype(BF)
            near_kv[piece, 1] = dv_acc[0, rows].astype(BF)
        for piece in reversed(pieces):
            direct_copy(OFFSETS[piece // 2], piece % 2).start()

    def send_query(chunk, pieces):
        first, last = pieces[0] * ROWS, (pieces[-1] + 1) * ROWS
        total = dq_acc[chunk, :, first:last].T
        if chunk == 0:
            own_q[...] = total[0:ROWS]
        total = total.astype(BF).reshape(len(pieces), ROWS, PAIR)
        send_q[chunk, pieces[0] : pieces[-1] + 1] = total
        for piece in reversed(pieces):
            if chunk or piece:
                query_copy(chunk, OFFSETS[piece // 2], piece % 2).start()

    whole(0, 0)
    pass_on(2)
    for chunk in (1, 2):
        prepare_k(chunk, NEAR)
        prepare_q(chunk, NEAR)
    tile([(1, NEAR), (2, NEAR)], [(0, WHOLE)])
    arrive(1, 1)
    tile([(1, REST)], [(0, WHOLE)])
    pass_on(3)
    arrive(0, 1)
    whole(1, 1)
    arrive(1, 2)
    tile([(2, REST)], [(0, WHOLE)])
    whole(2, 1)
    arrive(0, 2)
    whole(2, 2)
    whole(1, 2)
    arrive(0, 3, WHOLE)
    whole(1, 3)
    send_sums(1)
    whole(2, 3)
    send_sums(2)
    whole(0, 3)
    arrive(1, 3, WHOLE)
    whole(3, 3)
    send_query(3, range(8))
    whole(3, 0)
    send_query(0, range(8))
    whole(3, 1)
    whole(3, 2)
    send_sums(3)
    hop(1)
    whole(0, 1)
    send_query(1, range(8))
    hop(2)
    whole(0, 2)
    send_query(2, range(8))
    send_direct(range(1, 8))
    hop(3)

    def columns(offset, other):
        return pl.ds(pl.multiple_of(pair_at(offset, other) * PAIR, PAIR), PAIR)

    def own_sum(first, parts):
        for part in parts:
            first = first + part.astype(F32)
        return first.astype(BF)

    for side in range(2):
        near_all(side).wait_send()
        for chunk in FAR:
            cross_all(side, chunk).wait_send()
            ring_all(side, chunk).wait_send()
    for chunk in (0, 1, 3):
        query_all(chunk).wait_send()
    for chunk in FAR:
        for i in range(2):
            sum_all(chunk, i).wait_send()
    back_all().wait_send()

    back_all().wait_recv()
    for chunk in FAR:
        for other in (0, 1):
            cols = columns(-OFFSETS[chunk], other)
            piece = 2 * chunk + other
            out_ref[1, :, cols] = home_kv[piece, 0]
            out_ref[2, :, cols] = home_kv[piece, 1]
    for chunk in range(RING):
        query_all(chunk).wait_recv()
        for other in (0, 1):
            parts = [came_q[chunk, 2 * slot + other] for slot in range(RING)]
            first = parts[0].astype(F32) if chunk or other else own_q[...]
            out_ref[0, :, columns(-OFFSETS[chunk], other)] = own_sum(first, parts[1:])
    direct_all().wait_recv()
    for i, acc in enumerate((dk_acc, dv_acc)):
        for other in (0, 1):
            parts = [direct_kv[2 * slot + other, i] for slot in range(RING)]
            first = parts[0].astype(F32) if other else acc[0, 0:ROWS]
            out_ref[1 + i, :, columns(0, other)] = own_sum(first, parts[1:])
    direct_all().wait_send()
    query_all(2).wait_send()


def shards(queries, key_rows, value_rows, output_rows, grad_out, log_sums):
    vmem = pl.BlockSpec(memory_space=pltpu.VMEM)
    hbm = pl.BlockSpec(memory_space=pltpu.HBM)
    out = jax.ShapeDtypeStruct((ROWS, GROUP * PAIR), F32)
    dma = pltpu.SemaphoreType.DMA
    arrays = (queries, key_rows, value_rows, output_rows, grad_out, log_sums.T)
    r = pl.pallas_call(
        kernel,
        out_shape=jax.ShapeDtypeStruct((3, ROWS, GROUP * PAIR), BF),
        in_specs=[hbm] * 6,
        out_specs=vmem,
        scratch_shapes=[pltpu.VMEM((ROWS, GROUP * PAIR), BF)] * 5 + [
            pltpu.VMEM((2 * GROUP, ROWS), F32),
            dma((6,)),
            pltpu.VMEM((GROUP, SIDE, PAIR), BF),
            pltpu.VMEM((GROUP, 2 * ROWS, PAIR), BF),
            pltpu.VMEM((RING, GROUP, SIDE, PAIR), BF),
            pltpu.VMEM((RING, GROUP, 2 * ROWS, PAIR), BF),
            pltpu.VMEM((RING, 2, CHUNK, PAIR), BF),
            pltpu.VMEM((RING, 2, CHUNK, PAIR), BF),
            pltpu.VMEM((RING, PAIR, CHUNK), BF),
            pltpu.VMEM((RING, 8, CHUNK), F32),
            pltpu.VMEM((RING, PAIR, CHUNK), F32),
            pltpu.VMEM((RING, CHUNK, PAIR), F32),
            pltpu.VMEM((RING, CHUNK, PAIR), F32),
            pltpu.VMEM((RING, 2, RING, 2 * ROWS, PAIR), BF),
            pltpu.VMEM((RING, 2, RING, 2 * ROWS, PAIR), BF),
            pltpu.VMEM((GROUP, 2, ROWS, PAIR), BF),
            pltpu.VMEM((GROUP, 2, ROWS, PAIR), BF),
            pltpu.VMEM((GROUP, 2, ROWS, PAIR), BF),
            pltpu.VMEM((GROUP, 2, ROWS, PAIR), BF),
            pltpu.VMEM((RING, GROUP, ROWS, PAIR), BF),
            pltpu.VMEM((RING, GROUP, ROWS, PAIR), BF),
            pltpu.VMEM((ROWS, PAIR), F32),
            dma((2, 2)),
            dma((2, 2, RING)),
            dma((2, 2, RING)),
            dma((2, RING, 2)),
            dma((2,)),
            dma((2,)),
            dma((2, RING)),
        ],
        compiler_params=pltpu.CompilerParams(
            collective_id=0, has_side_effects=True, vmem_limit_bytes=48 * 2**20
        ),
        cost_estimate=pl.CostEstimate(
            flops=5 * 2**30, bytes_accessed=2**21, transcendentals=2**23
        ),
    )(*(pltpu.with_memory_space_constraint(array, pltpu.HBM) for array in arrays))
    return r[0].astype(F32), r[1].astype(F32), r[2].astype(F32)


def solution(mesh):
    q_side = P(("pb", "ka"), None)
    k_side = P(("ka", "pb"), None)
    return jax.shard_map(
        shards,
        mesh=mesh,
        in_specs=(q_side, k_side, k_side, q_side, q_side, q_side),
        out_specs=(q_side, k_side, k_side),
        check_vma=False,
    )
```
